256 devices in a mesh: row: 64 (over x, z, y_hi), rep: 4 (over y_lo, core).
Axes of the slice: x: 4, y: 4 (y_hi: 2, y_lo: 2; y = y_hi * 2 + y_lo), z: 8, core: 2. Of those that a mesh axis runs over, the one named last changes fastest.
Arguments:
- features: bfloat16 [4, 16384, 128], P('rep', 'row'), may hold values from -6 to 6
- weight: bfloat16 [128, 256], replicated, may hold values from -0.5 to 0.5
- bias_vector: float32 [256], replicated, may hold values from -3 to 3
- edge_tiles: bfloat16 [512, 4, 24, 128, 128], P('row', 'rep'), may hold values from -0.109375 to 0.109375
- tile_columns: int32 [512, 4, 24], P('row', 'rep'), may hold values from 0 to 127, as said below
- live_counts: int32 [512, 4], P('row', 'rep'), may hold values from 1 to 24, as said below
- cotangent: bfloat16 [65536, 256], P(('row', 'rep')), may hold values from -6 to 6
Outputs:
- hidden_out: bfloat16 [65536, 256], P(('row', 'rep'))
- feature_grad: bfloat16 [4, 16384, 128], P('rep', 'row')
- weight_grad: float32 [128, 256], replicated
- bias_grad: float32 [256], replicated
The draws below stay inside these ranges and needn't reach their ends.
Inputs may be any that keep to these rules, and one draw needn't show every extreme that they name: `tile_columns`: the slots of one block row and section name distinct column tiles. The first live_counts slots of a block row and section are live. On some row indices, row index 0 among them, every block row fills all 24 slots of every section; on the others no count passes 24 // 4.
All inputs are finite; a program needn't handle non-finite values.
Results may differ from the reference program's by a relative error of at most 0.0075.
Values may be sent and summed in bfloat16 or wider, within the bound.
No kernel may reach another device: no remote copies, remote signals or barrier semaphores. Data moves between devices by JAX's collectives and lax.ppermute only.
A program may use at most 128 MiB of HBM per device.

```python
import jax
import jax.numpy as jnp
from jax import lax

F = 128
HID = 256
TILE = 128
RB = 8
KS = 24
NT = 512
NTG = 128
NODES = 65536
N_REP = 4


def draw_tile_columns(key, part):
    key = jax.random.fold_in(key, 11)
    keys = jax.random.split(key, NT * N_REP)
    picks = jax.vmap(lambda single: jax.random.permutation(single, NTG)[:KS])(keys)
    return picks.reshape(NT, N_REP, KS).astype(jnp.int32)


def draw_live_counts(key, part):
    key = jax.random.fold_in(key, 23)
    light_key, heavy_key = jax.random.split(key)
    light = jax.random.randint(light_key, (NT, N_REP), 1, KS // 4 + 1)
    owners = NT // RB
    heavy_rows = jax.random.randint(heavy_key, (owners,), 0, 4) == 0
    heavy_rows = heavy_rows.at[0].set(True)
    heavy = jnp.repeat(heavy_rows, RB)[:, None]
    return jnp.where(heavy, KS, light).astype(jnp.int32)


def block_scale(stream_key, dims, cuts, smallest, top_value):
    level, own = 1.0, jax.random.fold_in(stream_key, 6)
    for position, blocks in cuts:
        draws = jnp.exp(jax.random.uniform(jax.random.fold_in(own, position), (blocks,), jnp.float32, smallest / len(cuts), top_value / len(cuts)))
        level = level * jnp.repeat(draws, dims[position] // blocks).reshape([-1 if axis == position else 1 for axis in range(len(dims))])
    return level


def bell_draw(own_key, dims, deviation, bound, cuts=(), kind=jnp.bfloat16):
    loudness = block_scale(own_key, dims, cuts, -0.22, 0.18) if cuts else 1.0
    values = jax.random.normal(own_key, dims, jnp.float32) * deviation * loudness
    return jnp.minimum(jnp.maximum(values, -bound), bound).astype(kind)


def setup_inputs(seed: int = 0) -> dict:
    arg_keys = jax.random.split(jax.random.key(seed), 8)
    features = bell_draw(arg_keys[0], (N_REP, NTG * TILE, F), 1.0, 6.0, ((0, 4), (1, 64)))
    weight = bell_draw(arg_keys[1], (F, HID), F ** -0.5, 0.5)
    bias_vector = bell_draw(arg_keys[2], (HID,), 0.5, 3.0, (), jnp.float32)
    edge_tiles = bell_draw(arg_keys[3], (NT, N_REP, KS, TILE, TILE), (TILE * KS) ** -0.5, 0.109375, ((0, 64), (1, 4)))
    tile_columns = draw_tile_columns(jax.random.fold_in(arg_keys[7], 71), 0)
    live_counts = draw_live_counts(jax.random.fold_in(arg_keys[7], 71), 0)
    cotangent = bell_draw(arg_keys[6], (NODES, HID), 1.0, 6.0, ((0, 256),))
    return dict(features=features, weight=weight, bias_vector=bias_vector, edge_tiles=edge_tiles, tile_columns=tile_columns, live_counts=live_counts, cotangent=cotangent)


def reference(features, weight, bias_vector, edge_tiles, tile_columns, live_counts, cotangent):
    projected = jnp.dot(features.reshape(-1, F), weight, preferred_element_type=jnp.float32).astype(jnp.bfloat16)
    projected = projected.reshape(N_REP, NTG, TILE, HID)
    slot_ids = lax.broadcasted_iota(jnp.int32, (N_REP, KS), 1)
    group_ids = jnp.arange(N_REP)[:, None]

    def masked_row(row_index):
        live_mask = slot_ids < live_counts[row_index][:, None]
        return jnp.where(live_mask[:, :, None, None], edge_tiles[row_index].astype(jnp.float32), jnp.float32(0.0))

    def forward_row(row_index):
        masked = masked_row(row_index)
        picked = projected[group_ids, tile_columns[row_index]].astype(jnp.float32)
        return jnp.einsum('gskb,gsbf->kf', masked, picked)

    aggregate = lax.map(forward_row, jnp.arange(NT)).reshape(NT * TILE, HID)
    preact = aggregate + bias_vector
    gate_value = jax.nn.sigmoid(preact)
    hidden_out = (preact * gate_value).astype(jnp.bfloat16)
    outgrad = (cotangent.astype(jnp.float32) * gate_value * (1.0 + preact * (1.0 - gate_value))).astype(jnp.bfloat16)
    outgrad_tiles = outgrad.reshape(NT, TILE, HID)

    def backward_row(totals, row_index):
        masked = masked_row(row_index)
        contrib = jnp.einsum('gskb,kf->gsbf', masked, outgrad_tiles[row_index].astype(jnp.float32))
        return totals.at[group_ids, tile_columns[row_index]].add(contrib), None

    totals, unused = lax.scan(backward_row, jnp.zeros((N_REP, NTG, TILE, HID), jnp.float32), jnp.arange(NT))
    projected_grad = totals.reshape(N_REP * NTG * TILE, HID)
    feature_grad = jnp.dot(projected_grad, weight.astype(jnp.float32).T, precision=lax.Precision.HIGHEST)
    feature_grad = feature_grad.astype(jnp.bfloat16).reshape(N_REP, NTG * TILE, F)
    weight_grad = jnp.dot(features.reshape(-1, F).astype(jnp.float32).T, projected_grad, precision=lax.Precision.HIGHEST)
    bias_grad = jnp.sum(outgrad.astype(jnp.float32), axis=0)
    return hidden_out, feature_grad, weight_grad, bias_grad
```

```python
import functools

import jax
import jax.numpy as jnp
from jax import lax
from jax.experimental import pallas as pl
from jax.experimental.pallas import tpu as pltpu
from jax.sharding import PartitionSpec as P

NX, NZ, NY = 4, 8, 2
TILE = 128
GROUP = 6
BF = jnp.bfloat16
F32 = jnp.float32
VMEM = pltpu.VMEM
SMEM = pltpu.SMEM


def row_perm(dx=0, dz=0, dy=0, flip=0):
    pairs = []
    for x in range(NX):
        for z in range(NZ):
            for y in range(NY):
                if flip:
                    tx, tz = x ^ dx, z ^ dz
                else:
                    tx, tz = (x + dx) % NX, (z + dz) % NZ
                ty = (y + dy) % NY
                pairs.append(((x * NZ + z) * NY + y, (tx * NZ + tz) * NY + ty))
    return pairs


def send(value, dx=0, dz=0, dy=0, flip=0):
    return lax.ppermute(value, "row", row_perm(dx, dz, dy, flip))


def swap(value, bit):
    return lax.ppermute(value, "rep", [(i, i ^ bit) for i in range(4)])


def forward_kernel(places, count_ref, pos_ref, edge_ref, *rest):
    pieces = rest[: len(places)]
    out_ref, table, sems = rest[len(places):]
    step = pl.program_id(0)

    @pl.when(step == 0)
    def _():
        copies = []
        for i, (start, size) in enumerate(places):
            copies.append(pltpu.make_async_copy(pieces[i], table.at[pl.ds(start, size)], sems.at[i]))
        for copy in copies:
            copy.start()
        for copy in copies:
            copy.wait()

    count = count_ref[step]
    slots = edge_ref.shape[2]

    def body(g, acc):
        left, right = [], []
        for i in range(GROUP):
            s = g * GROUP + i
            tile = edge_ref[0, 0, s]
            left.append(jnp.where(s < count, tile, jnp.zeros_like(tile)))
            right.append(table[pos_ref[step * slots + s]])
        return acc + jnp.dot(
            jnp.concatenate(left, axis=1), jnp.concatenate(right, axis=0), preferred_element_type=F32
        )

    groups = (count + (GROUP - 1)) // GROUP
    acc = lax.fori_loop(0, groups, body, jnp.zeros((TILE, TILE), F32))
    out_ref[0] = acc.astype(out_ref.dtype)


def forward(counts, positions, edge_tiles, pieces):
    places = tuple((start, piece.shape[0]) for start, piece in pieces)
    arrays = [piece for _, piece in pieces]
    rows, _, slots = edge_tiles.shape[:3]
    return pl.pallas_call(
        functools.partial(forward_kernel, places),
        grid=(rows,),
        out_shape=jax.ShapeDtypeStruct((rows, TILE, TILE), BF),
        in_specs=[
            pl.BlockSpec(memory_space=SMEM),
            pl.BlockSpec(memory_space=SMEM),
            pl.BlockSpec((1, 1, slots, TILE, TILE), lambda t: (t, 0, 0, 0, 0)),
        ]
        + [pl.BlockSpec(memory_space=pl.ANY)] * len(arrays),
        out_specs=pl.BlockSpec((1, TILE, TILE), lambda t: (t, 0, 0)),
        scratch_shapes=[VMEM((2 * NX * NZ * NY, TILE, TILE), BF), pltpu.SemaphoreType.DMA((len(arrays),))],
        compiler_params=pltpu.CompilerParams(vmem_limit_bytes=32 * 2**20),
        name="forward",
    )(counts, positions, edge_tiles, *arrays)


def middle_kernel(rep_ref, part_ref, weight_ref, bias_ref, cot_ref, hidden_ref, slope_ref, grad_ref):
    agg = part_ref[0].astype(F32)
    for i in range(1, part_ref.shape[0]):
        agg = agg + part_ref[i].astype(F32)
    weight = weight_ref[...]
    preact = (
        jnp.dot(agg, weight.astype(F32), preferred_element_type=F32, precision=lax.Precision.HIGHEST)
        + bias_ref[...]
    )
    gate = jax.nn.sigmoid(preact)
    hidden_ref[...] = (preact * gate).astype(BF)
    outgrad = (cot_ref[...].astype(F32) * gate * (1.0 + preact * (1.0 - gate))).astype(BF)
    slope = lax.dot_general(weight, outgrad, (((1,), (1,)), ((), ())), preferred_element_type=F32).astype(BF)
    for i in range(slope_ref.shape[0]):
        slope_ref[i] = slope[:, i * TILE:(i + 1) * TILE]
    wide = outgrad.astype(F32)
    grad = lax.dot_general(
        agg, wide, (((0,), (0,)), ((), ())), preferred_element_type=F32, precision=lax.Precision.HIGHEST
    )
    bias = jnp.sum(wide, axis=0, keepdims=True)
    me = rep_ref[0]
    first = lax.broadcasted_iota(jnp.int32, (8, bias.shape[1]), 0) == 0
    for q in range(4):
        where = me ^ q
        grad_ref[where, 0:32, :] = grad[q * 32:(q + 1) * 32]
        if q == 0:
            grad_ref[where, 32:40, :] = jnp.where(first, jnp.broadcast_to(bias, first.shape), 0.0)
        else:
            grad_ref[where, 32:40, :] = jnp.zeros(first.shape, F32)


def middle(me, parts, weight, bias, cotangent):
    nodes, width = cotangent.shape
    vmem = pl.BlockSpec(memory_space=VMEM)
    return pl.pallas_call(
        middle_kernel,
        out_shape=(
            jax.ShapeDtypeStruct((nodes, width), BF),
            jax.ShapeDtypeStruct((nodes // TILE, TILE, TILE), BF),
            jax.ShapeDtypeStruct((4, 40, width), F32),
        ),
        in_specs=[pl.BlockSpec(memory_space=SMEM)] + [vmem] * 4,
        out_specs=(vmem, vmem, vmem),
        compiler_params=pltpu.CompilerParams(vmem_limit_bytes=32 * 2**20),
        name="middle",
    )(me, parts, weight, bias.reshape(1, -1), cotangent)


def backward_kernel(places, count_ref, pos_ref, edge_ref, slope_ref, *rest):
    outs, totals = rest[:-1], rest[-1]
    step = pl.program_id(0)

    @pl.when(step == 0)
    def _():
        def clear(i, carry):
            totals[pl.ds(i * 8, 8)] = jnp.zeros((8, TILE, TILE), F32)
            return carry

        lax.fori_loop(0, totals.shape[0] // 8, clear, 0)

    count = count_ref[step]
    slots = edge_ref.shape[2]
    slope = slope_ref[step]

    def body(g, carry):
        tiles, where = [], []
        for i in range(GROUP):
            s = g * GROUP + i
            tile = edge_ref[0, 0, s]
            tiles.append(jnp.where(s < count, tile, jnp.zeros_like(tile)))
            where.append(pos_ref[step * slots + s])
        terms = jnp.dot(slope, jnp.concatenate(tiles, axis=1), preferred_element_type=F32)
        old = [totals[w] for w in where]
        for i in range(GROUP):
            totals[where[i]] = old[i] + terms[:, i * TILE:(i + 1) * TILE]
        return carry

    lax.fori_loop(0, (count + (GROUP - 1)) // GROUP, body, 0)

    @pl.when(step == pl.num_programs(0) - 1)
    def _():
        for out, (start, size) in zip(outs, places):
            def store(i, carry, out=out, start=start):
                out[i] = totals[start + i].astype(out.dtype)
                return carry

            lax.fori_loop(0, size, store, 0)


def backward(counts, positions, edge_tiles, slope, places):
    rows, _, slots = edge_tiles.shape[:3]
    whole = lambda t: (0, 0, 0)
    return pl.pallas_call(
        functools.partial(backward_kernel, places),
        grid=(rows,),
        out_shape=tuple(jax.ShapeDtypeStruct((size, TILE, TILE), BF) for _, size in places),
        in_specs=[
            pl.BlockSpec(memory_space=SMEM),
            pl.BlockSpec(memory_space=SMEM),
            pl.BlockSpec((1, 1, slots, TILE, TILE), lambda t: (t, 0, 0, 0, 0)),
            pl.BlockSpec(slope.shape, whole),
        ],
        out_specs=tuple(pl.BlockSpec((size, TILE, TILE), whole) for _, size in places),
        scratch_shapes=[VMEM((2 * NX * NZ * NY, TILE, TILE), F32)],
        compiler_params=pltpu.CompilerParams(vmem_limit_bytes=40 * 2**20),
        name="backward",
    )(counts, positions, edge_tiles, slope)


def last_kernel(own_ref, got_ref, quarter_ref, feature_ref, weight_ref, bias_ref):
    for i in range(2):
        total = own_ref[i].astype(F32) + got_ref[i].astype(F32)
        feature_ref[0, i * TILE:(i + 1) * TILE, :] = total.T.astype(BF)
    for q in range(4):
        weight_ref[q * 32:(q + 1) * 32, :] = quarter_ref[q, 0:32, :]
    bias_ref[...] = quarter_ref[0, 32:33, :]


def last(own, got, quarters):
    width = quarters.shape[-1]
    vmem = pl.BlockSpec(memory_space=VMEM)
    return pl.pallas_call(
        last_kernel,
        out_shape=(
            jax.ShapeDtypeStruct((1, 2 * TILE, TILE), BF),
            jax.ShapeDtypeStruct((TILE, width), F32),
            jax.ShapeDtypeStruct((1, width), F32),
        ),
        in_specs=[vmem] * 3,
        out_specs=(vmem, vmem, vmem),
        name="last",
    )(own, got, quarters)


def add(*values):
    total = values[0].astype(F32)
    for value in values[1:]:
        total = total + value.astype(F32)
    return total.astype(BF)


def gather_features(own):
    other = send(own, dy=1)
    a = jnp.stack([own[0], other[0]])
    b = jnp.stack([own[1], other[1]])
    a1, a2, a3 = send(a, dx=1), send(a, dx=2), send(a, dx=-1)
    lo, hi = jnp.concatenate([a, a1]), jnp.concatenate([a2, a3])
    pieces = [(0, lo), (4, hi)]
    up_lo, up_hi, down_lo, down_hi = lo, hi, lo, hi
    bu, bd = b, b
    zs = {0: b}
    for k in (1, 2, 3, 4):
        up_lo, down_hi = send(up_lo, dz=1), send(down_hi, dz=-1)
        pieces += [(8 * k, up_lo), (8 * (8 - k) + 4, down_hi)]
        if k < 4:
            up_hi, down_lo = send(up_hi, dz=1), send(down_lo, dz=-1)
            pieces += [(8 * k + 4, up_hi), (8 * (8 - k), down_lo)]
            bu, bd = send(bu, dz=1), send(bd, dz=-1)
            zs[k], zs[8 - k] = bu, bd
        else:
            zs[4] = send(bu, dz=1)
    wide = jnp.concatenate([zs[k] for k in range(8)])
    pieces.append((64, wide))
    for k, hop in ((1, 1), (2, 2), (3, -1)):
        pieces.append((64 + 16 * k, send(wide, dx=hop)))
    return pieces


A_PLACES = tuple((8 * k + 4 * h, 4) for k in range(8) for h in range(2))
B_PLACES = tuple((64 + 16 * k, 16) for k in range(4))


def scatter_totals(parts):
    a = {(k, h): parts[2 * k + h] for k in range(8) for h in range(2)}
    b = parts[16:]
    got = [send(b[1], dx=1), send(b[2], dx=2), send(b[3], dx=-1)]
    up = {0: a[4, 0], 1: a[3, 1]}
    down = {1: a[4, 1], 0: a[5, 0]}
    up[0] = add(send(up[0], dz=1), a[3, 0])
    down[1] = add(send(down[1], dz=-1), a[5, 1])
    for k in (3, 2, 1):
        for h in (0, 1):
            moved = send(up[h], dz=1)
            up[h] = add(moved, a[k - 1, h]) if k > 1 else moved
            moved = send(down[h], dz=-1)
            down[h] = add(moved, a[9 - k, h]) if k > 1 else moved
    lo, hi = add(a[0, 0], up[0], down[0]), add(a[0, 1], up[1], down[1])
    ax = [lo[:2], send(lo[2:], dx=1), send(hi[:2], dx=2), send(hi[2:], dx=-1)]
    own_a = add(*ax)
    bz = add(b[0], *got)
    bz = [bz[2 * k:2 * k + 2] for k in range(8)]
    u, d = send(bz[4], dz=1), bz[5]
    u = add(u, bz[3])
    for k in (3, 2, 1):
        u, d = send(u, dz=1), send(d, dz=-1)
        if k > 1:
            u, d = add(u, bz[k - 1]), add(d, bz[9 - k])
    own_b = add(bz[0], u, d)
    mine = jnp.stack([own_a[0], own_b[0]])
    theirs = send(jnp.stack([own_a[1], own_b[1]]), dy=1)
    return mine, theirs


def all_reduce(grad):
    got = swap(jnp.stack([grad[1], grad[3]]), 1)
    near, far = grad[0] + got[0], grad[2] + got[1]
    value = near + swap(far, 2)
    value = value + send(value, dy=1)
    for bit in (1, 2):
        value = value + send(value, dx=bit, flip=1)
    for bit in (1, 2, 4):
        value = value + send(value, dz=bit, flip=1)
    return lax.all_gather(value, "rep", axis=0)


def shards(features, weight, bias_vector, edge_tiles, tile_columns, live_counts, cotangent):
    row, rep = lax.axis_index("row"), lax.axis_index("rep")
    x, z, y = row // (NZ * NY), (row // NY) % NZ, row % NY
    columns = tile_columns.reshape(-1)
    owner, which = columns // 2, columns % 2
    ox, oz, oy = owner // (NZ * NY), (owner // NY) % NZ, owner % NY
    dy = oy ^ y

    def places(dx, dz):
        return jnp.where(which == 0, (dz * NX + dx) * 2 + dy, 64 + (dx * NZ + dz) * 2 + dy).astype(jnp.int32)

    behind = places((x - ox) % NX, (z - oz) % NZ)
    ahead = places((ox - x) % NX, (oz - z) % NZ)
    counts = live_counts.reshape(-1)

    with jax.named_scope("gather"):
        pieces = gather_features(features.reshape(2, TILE, TILE))
    partial = forward(counts, behind, edge_tiles, pieces)
    with jax.named_scope("sections"):
        parts = lax.all_to_all(partial.reshape(4, 2 * TILE, TILE), "rep", 0, 0, tiled=True)
    hidden_out, slope, grad = middle(rep.reshape(1), parts, weight, bias_vector, cotangent)
    with jax.named_scope("slopes"):
        slopes = lax.all_gather(slope, "rep", axis=0, tiled=True)
    totals = backward(counts, ahead, edge_tiles, slopes, A_PLACES + B_PLACES)
    with jax.named_scope("weights"):
        quarters = all_reduce(grad)
    with jax.named_scope("scatter"):
        mine, theirs = scatter_totals(totals)
    feature_grad, weight_grad, bias_grad = last(mine, theirs, quarters)
    return hidden_out, feature_grad, weight_grad, bias_grad.reshape(-1)


def solution(mesh):
    in_specs = (
        P("rep", "row", None),
        P(),
        P(),
        P("row", "rep", None, None, None),
        P("row", "rep", None),
        P("row", "rep"),
        P(("row", "rep"), None),
    )
    out_specs = (P(("row", "rep"), None), P("rep", "row", None), P(), P())
    return jax.shard_map(shards, mesh=mesh, in_specs=in_specs, out_specs=out_specs, check_vma=False)
```

```python
import functools

import jax
import jax.numpy as jnp
from jax import lax
from jax.experimental import pallas as pl
from jax.experimental.pallas import tpu as pltpu
from jax.sharding import Mesh
from jax.sharding import PartitionSpec as P

NX, NZ, NY = 4, 8, 2
TILE = 128
GROUP = 6
BF = jnp.bfloat16
F32 = jnp.float32
VMEM = pltpu.VMEM
SMEM = pltpu.SMEM


def shift_x(value, k):
    return lax.ppermute(value, "x", [(i, (i + k) % NX) for i in range(NX)])


def shift_z(value, k):
    return lax.ppermute(value, "z", [(i, (i + k) % NZ) for i in range(NZ)])


def swap(value, *axes):
    pairs = [(i, (1 << len(axes)) - 1 - i) for i in range(1 << len(axes))]
    return lax.ppermute(value, axes, pairs)


def add32(*values):
    total = values[0].astype(F32)
    for value in values[1:]:
        total = total + value.astype(F32)
    return total


def add(*values):
    return add32(*values).astype(BF)


def forward_kernel(places, rep_ref, count_ref, pos_ref, edge_ref, *rest):
    pieces = rest[: len(places)]
    outs = rest[len(places):-2]
    table, sems = rest[-2:]
    step = pl.program_id(0)

    @pl.when(step == 0)
    def _():
        copies = []
        for i, (start, size) in enumerate(places):
            copies.append(pltpu.make_async_copy(pieces[i], table.at[pl.ds(start, size)], sems.at[i]))
        for copy in copies:
            copy.start()
        for copy in copies:
            copy.wait()

    count = count_ref[step]
    slots = edge_ref.shape[2]

    def body(g, acc):
        left, right = [], []
        for i in range(GROUP):
            s = g * GROUP + i
            tile = edge_ref[0, 0, s]
            left.append(jnp.where(s < count, tile, jnp.zeros_like(tile)))
            right.append(table[pos_ref[step * slots + s]])
        return acc + jnp.dot(
            jnp.concatenate(left, axis=1), jnp.concatenate(right, axis=0), preferred_element_type=F32
        )

    groups = (count + (GROUP - 1)) // GROUP
    acc = lax.fori_loop(0, groups, body, jnp.zeros((TILE, TILE), F32))
    for q in range(len(outs)):

        @pl.when((step // 2) ^ rep_ref[0] == q)
        def _(q=q):
            outs[q][step % 2] = acc.astype(BF)


def forward(rep, counts, positions, edge_tiles, pieces):
    places = tuple((start, piece.shape[0]) for start, piece in pieces)
    arrays = [piece for _, piece in pieces]
    rows, _, slots = edge_tiles.shape[:3]
    return pl.pallas_call(
        functools.partial(forward_kernel, places),
        grid=(rows,),
        out_shape=(jax.ShapeDtypeStruct((2, TILE, TILE), BF),) * 4,
        in_specs=[pl.BlockSpec(memory_space=SMEM)] * 3
        + [pl.BlockSpec((1, 1, slots, TILE, TILE), lambda t: (t, 0, 0, 0, 0))]
        + [pl.BlockSpec(memory_space=pl.ANY)] * len(arrays),
        out_specs=(pl.BlockSpec((2, TILE, TILE), lambda t: (0, 0, 0)),) * 4,
        scratch_shapes=[VMEM((2 * NX * NZ * NY, TILE, TILE), BF), pltpu.SemaphoreType.DMA((len(arrays),))],
        compiler_params=pltpu.CompilerParams(vmem_limit_bytes=56 * 2**20),
        name="forward",
    )(rep, counts, positions, edge_tiles, *arrays)


def middle_kernel(rep_ref, p0, p1, p2, p3, weight_ref, bias_ref, cot_ref, hidden_ref, slope_ref, near_ref, pair_ref, far_ref):
    agg = add32(*[jnp.concatenate([p[0], p[1]], axis=0) for p in (p0, p1, p2, p3)])
    weight = weight_ref[...]
    preact = (
        jnp.dot(agg, weight.astype(F32), preferred_element_type=F32, precision=lax.Precision.HIGHEST)
        + bias_ref[...]
    )
    gate = jax.nn.sigmoid(preact)
    hidden_ref[...] = (preact * gate).astype(BF)
    outgrad = (cot_ref[...].astype(F32) * gate * (1.0 + preact * (1.0 - gate))).astype(BF)
    slope = lax.dot_general(weight, outgrad, (((1,), (1,)), ((), ())), preferred_element_type=F32).astype(BF)
    for i in range(slope_ref.shape[0]):
        slope_ref[i] = slope[:, i * TILE:(i + 1) * TILE]
    wide = outgrad.astype(F32)
    grad = lax.dot_general(
        agg, wide, (((0,), (0,)), ((), ())), preferred_element_type=F32, precision=lax.Precision.HIGHEST
    )
    bias = jnp.sum(wide, axis=0, keepdims=True)
    places = (near_ref, (pair_ref, 0), far_ref, (pair_ref, 1))
    for q in range(4):
        if q % 2:
            ref = places[q][0].at[places[q][1]]
        else:
            ref = places[q]
        for p in range(4):

            @pl.when(rep_ref[0] ^ q == p)
            def _(ref=ref, p=p):
                ref[0:32, :] = grad[p * 32:(p + 1) * 32, 0:TILE]
                ref[32:64, :] = grad[p * 32:(p + 1) * 32, TILE:]

        ref[64:72, :] = jnp.broadcast_to(bias[:, 0:TILE], (8, TILE))
        ref[72:80, :] = jnp.broadcast_to(bias[:, TILE:], (8, TILE))


def middle(rep, parts, weight, bias, cotangent):
    nodes, width = cotangent.shape
    vmem = pl.BlockSpec(memory_space=VMEM)
    quarter = jax.ShapeDtypeStruct((80, TILE), F32)
    return pl.pallas_call(
        middle_kernel,
        out_shape=(
            jax.ShapeDtypeStruct((nodes, width), BF),
            jax.ShapeDtypeStruct((nodes // TILE, TILE, TILE), BF),
            quarter,
            jax.ShapeDtypeStruct((2, 80, TILE), F32),
            quarter,
        ),
        in_specs=[pl.BlockSpec(memory_space=SMEM)] + [vmem] * 7,
        out_specs=(vmem,) * 5,
        compiler_params=pltpu.CompilerParams(vmem_limit_bytes=32 * 2**20),
        name="middle",
    )(rep, *parts, weight, bias.reshape(1, -1), cotangent)


def backward_kernel(places, count_ref, pos_ref, edge_ref, slope_ref, *rest):
    outs, totals = rest[:-1], rest[-1]
    step = pl.program_id(0)

    @pl.when(step == 0)
    def _():
        def clear(i, carry):
            totals[pl.ds(i * 8, 8)] = jnp.zeros((8, TILE, TILE), F32)
            return carry

        lax.fori_loop(0, totals.shape[0] // 8, clear, 0)

    count = count_ref[step]
    slots = edge_ref.shape[2]
    slope = slope_ref[step]

    def body(g, carry):
        tiles, where = [], []
        for i in range(GROUP):
            s = g * GROUP + i
            tile = edge_ref[0, 0, s]
            tiles.append(jnp.where(s < count, tile, jnp.zeros_like(tile)))
            where.append(pos_ref[step * slots + s])
        terms = jnp.dot(slope, jnp.concatenate(tiles, axis=1), preferred_element_type=F32)
        old = [totals[w] for w in where]
        for i in range(GROUP):
            totals[where[i]] = old[i] + terms[:, i * TILE:(i + 1) * TILE]
        return carry

    lax.fori_loop(0, (count + (GROUP - 1)) // GROUP, body, 0)

    @pl.when(step == pl.num_programs(0) - 1)
    def _():
        for out, (start, size) in zip(outs, places):
            def store(i, carry, out=out, start=start):
                out[i] = totals[start + i].astype(out.dtype)
                return carry

            lax.fori_loop(0, size, store, 0)


def backward(counts, positions, edge_tiles, slope, places):
    rows, _, slots = edge_tiles.shape[:3]
    whole = lambda t: (0, 0, 0)
    return pl.pallas_call(
        functools.partial(backward_kernel, places),
        grid=(rows,),
        out_shape=tuple(jax.ShapeDtypeStruct((size, TILE, TILE), BF) for _, size in places),
        in_specs=[
            pl.BlockSpec(memory_space=SMEM),
            pl.BlockSpec(memory_space=SMEM),
            pl.BlockSpec((1, 1, slots, TILE, TILE), lambda t: (t, 0, 0, 0, 0)),
            pl.BlockSpec(slope.shape, whole),
        ],
        out_specs=tuple(pl.BlockSpec((size, TILE, TILE), whole) for _, size in places),
        scratch_shapes=[VMEM((2 * NX * NZ * NY, TILE, TILE), F32)],
        compiler_params=pltpu.CompilerParams(vmem_limit_bytes=56 * 2**20),
        name="backward",
    )(counts, positions, edge_tiles, slope)


def last_kernel(own_ref, got_ref, quarter_ref, feature_ref, weight_ref, bias_ref):
    for i in range(2):
        total = own_ref[i] + got_ref[i].astype(F32)
        feature_ref[0, i * TILE:(i + 1) * TILE, :] = total.T.astype(BF)
    for q in range(4):
        weight_ref[q * 32:(q + 1) * 32, 0:TILE] = quarter_ref[q, 0:32, :]
        weight_ref[q * 32:(q + 1) * 32, TILE:] = quarter_ref[q, 32:64, :]
    bias_ref[:, 0:TILE] = quarter_ref[0, 64:65, :]
    bias_ref[:, TILE:] = quarter_ref[0, 72:73, :]


def last(own, got, quarters):
    vmem = pl.BlockSpec(memory_space=VMEM)
    return pl.pallas_call(
        last_kernel,
        out_shape=(
            jax.ShapeDtypeStruct((1, 2 * TILE, TILE), BF),
            jax.ShapeDtypeStruct((TILE, 2 * TILE), F32),
            jax.ShapeDtypeStruct((1, 2 * TILE), F32),
        ),
        in_specs=[vmem] * 3,
        out_specs=(vmem, vmem, vmem),
        name="last",
    )(own, got, quarters)


def gather_features(own):
    other = swap(own, "y")
    base = jnp.concatenate([own, other[:1]])
    spread = jnp.broadcast_to(other[None, 1], (NZ, TILE, TILE))
    line = lax.all_to_all(spread, "z", 0, 0, tiled=True)
    plane = jnp.concatenate([base, shift_x(base, 1), shift_x(base, 2), shift_x(base, -1)])
    pieces = [(0, plane), (96, line)]
    for k, hop in ((1, 1), (2, 2), (3, -1)):
        pieces.append((96 + 8 * k, shift_x(line, hop)))
    up = down = plane
    for k in (1, 2, 3):
        up, down = shift_z(up, 1), shift_z(down, -1)
        pieces += [(12 * k, up), (12 * (8 - k), down)]
    pieces += [(48, shift_z(up[:6], 1)), (54, shift_z(down[6:], -1))]
    return pieces


A_PLACES = ((48, 6), (54, 6)) + tuple((12 * k, 12) for k in (3, 5, 2, 6, 1, 7, 0))
B_PLACES = tuple((96 + 8 * k, 8) for k in range(4))


def split(value):
    high = lax.reduce_precision(value, 8, 7)
    return jnp.concatenate([high.astype(BF), (value - high).astype(BF)])


def join(value):
    half = value.shape[0] // 2
    return value[:half].astype(F32) + value[half:].astype(F32)


def scatter_totals(parts, grad):
    rows = [p.reshape(-1, TILE) for p in parts]
    up, down = rows[0], rows[1]
    ups, downs = [None, rows[2], rows[4], rows[6]], [None, rows[3], rows[5], rows[7]]
    b = rows[9:]
    got_b = [shift_x(b[1], 1), shift_x(b[2], 2), shift_x(b[3], -1)]
    half, full = 6 * TILE, 12 * TILE
    wide = split(grad)
    grads = [grad]
    ride_up = ride_down = wide
    for step in range(4):
        up = shift_z(jnp.concatenate([up, ride_up]), 1)
        if step < 3:
            down = shift_z(jnp.concatenate([down, ride_down]), -1)
            size = half if step == 0 else full
            ride_up, ride_down = up[size:], down[size:]
            grads += [join(ride_up), join(ride_down)]
            up, down = up[:size], down[:size]
            if step == 0:
                up = jnp.concatenate([add(up, ups[1][:half]), ups[1][half:]])
                down = jnp.concatenate([downs[1][:half], add(down, downs[1][half:])])
            else:
                up, down = add(up, ups[step + 1]), add(down, downs[step + 1])
        else:
            down = shift_z(down, -1)
            grads.append(join(up[full:]))
            up = up[:full]
    line = add(b[0], *got_b)
    line = lax.all_to_all(line.reshape(NZ, TILE, TILE), "z", 0, 0, tiled=True)
    grad = add32(*grads)
    wide = split(grad)
    part = 3 * TILE
    total = add32(rows[8], up, down)
    sent = [total[k * part:(k + 1) * part].astype(BF) for k in (1, 2, 3)]
    got = [shift_x(jnp.concatenate([v, wide]), hop) for v, hop in zip(sent, (1, 2, -1))]
    total = add32(total[:part], *[g[:part] for g in got])
    grad = add32(grad, *[join(g[part:]) for g in got])
    last_b = add(*[line[k] for k in range(NZ)])
    theirs = swap(jnp.concatenate([total[2 * TILE:].astype(BF), last_b]), "y")
    return total[:2 * TILE].reshape(2, TILE, TILE), theirs.reshape(2, TILE, TILE), grad


def shards(features, weight, bias_vector, edge_tiles, tile_columns, live_counts, cotangent):
    x, z, y = lax.axis_index("x"), lax.axis_index("z"), lax.axis_index("y")
    rep = (lax.axis_index("near") * 2 + lax.axis_index("core")).reshape(1)
    columns = tile_columns.reshape(-1)
    owner, which = columns // 2, columns % 2
    ox, oz, oy = owner // (NZ * NY), (owner // NY) % NZ, owner % NY
    kind = (oy ^ y) * 2 + which

    def places(dx, dz):
        return jnp.where(kind < 3, (dz * NX + dx) * 3 + kind, 96 + dx * NZ + oz).astype(jnp.int32)

    behind = places((x - ox) % NX, (z - oz) % NZ)
    ahead = places((ox - x) % NX, (oz - z) % NZ)
    counts = live_counts.reshape(-1)

    with jax.named_scope("gather"):
        pieces = gather_features(features.reshape(2, TILE, TILE))
    partial = forward(rep, counts, behind, edge_tiles, pieces)
    with jax.named_scope("sections"):
        parts = [
            partial[0],
            swap(partial[1], "core"),
            swap(partial[2], "near"),
            swap(partial[3], "near", "core"),
        ]
    hidden_out, slope, near, pair, far = middle(rep, parts, weight, bias_vector, cotangent)
    with jax.named_scope("slopes"):
        slopes = lax.all_gather(slope, ("near", "core"), axis=0, tiled=True)
    with jax.named_scope("weights"):
        pair = swap(pair, "core")
        near, far = near + pair[0], far + pair[1]
        grad = near + swap(far, "near") + swap(near, "y") + swap(far, "y", "near")
    totals = backward(counts, ahead, edge_tiles, slopes, A_PLACES + B_PLACES)
    with jax.named_scope("scatter"):
        mine, theirs, grad = scatter_totals(totals, grad)
        quarters = lax.all_gather(grad, ("near", "core"), axis=0)
    feature_grad, weight_grad, bias_grad = last(mine, theirs, quarters)
    return hidden_out, feature_grad, weight_grad, bias_grad.reshape(-1)


def solution(mesh):
    grid = Mesh(mesh.devices.reshape(NX, NZ, NY, 2, 2), ("x", "z", "y", "near", "core"))
    row, rep = ("x", "z", "y"), ("near", "core")
    in_specs = (
        P(rep, row, None),
        P(),
        P(),
        P(row, rep, None, None, None),
        P(row, rep, None),
        P(row, rep),
        P(row + rep, None),
    )
    out_specs = (P(row + rep, None), P(rep, row, None), P(), P())
    return jax.shard_map(shards, mesh=grid, in_specs=in_specs, out_specs=out_specs, check_vma=False)
```

```python
import functools

import jax
import jax.numpy as jnp
from jax import lax
from jax.experimental import pallas as pl
from jax.experimental.pallas import tpu as pltpu
from jax.sharding import Mesh
from jax.sharding import PartitionSpec as P

NX, NZ, NY = 4, 8, 2
TILE = 128
GROUP = 6
BF = jnp.bfloat16
F32 = jnp.float32
VMEM = pltpu.VMEM
SMEM = pltpu.SMEM


def shift_x(value, k):
    return lax.ppermute(value, "x", [(i, (i + k) % NX) for i in range(NX)])


def shift_z(value, k):
    return lax.ppermute(value, "z", [(i, (i + k) % NZ) for i in range(NZ)])


def swap(value, *axes):
    pairs = [(i, (1 << len(axes)) - 1 - i) for i in range(1 << len(axes))]
    return lax.ppermute(value, axes, pairs)


def add32(*values):
    total = values[0].astype(F32)
    for value in values[1:]:
        total = total + value.astype(F32)
    return total


def add(*values):
    return add32(*values).astype(BF)


def each_row(count_ref, edge_ref, body):
    rows, _, slots = edge_ref.shape[:3]

    def row(t, carry):
        count = count_ref[t]

        @pl.when(count > GROUP)
        def _():
            body(t, count, slots)

        @pl.when(count <= GROUP)
        def _():
            body(t, count, GROUP)

        return carry

    lax.fori_loop(0, rows, row, 0)


def live_tile(edges, t, s, count):
    tile = edges[t, 0, s]
    return jnp.where(s < count, tile, jnp.zeros_like(tile))


def forward_kernel(places, rep_ref, count_ref, pos_ref, edges, *rest):
    pieces = rest[: len(places)]
    outs, table = rest[len(places):-1], rest[-1]
    slots = edges.shape[2]
    for piece, (place, size) in zip(pieces, places):

        def copy(i, carry, piece=piece, place=place):
            table[pl.ds(place + i * 4, 4)] = piece[pl.ds(i * 4, 4)]
            return carry

        lax.fori_loop(0, size // 4, copy, 0)

    def body(t, count, size):
        left = [live_tile(edges, t, s, count) for s in range(size)]
        right = [table[pos_ref[t * slots + s]] for s in range(size)]
        total = jnp.dot(
            jnp.concatenate(left, axis=1), jnp.concatenate(right, axis=0), preferred_element_type=F32
        ).astype(BF)
        for q in range(len(outs)):

            @pl.when((t // 2) ^ rep_ref[0] == q)
            def _(q=q):
                outs[q][t % 2] = total

    each_row(count_ref, edges, body)


def forward(rep, counts, positions, edge_tiles, pieces):
    places = tuple((place, piece.shape[0]) for place, piece in pieces)
    arrays = [piece for _, piece in pieces]
    rows, _, slots = edge_tiles.shape[:3]
    vmem = pl.BlockSpec(memory_space=VMEM)
    return pl.pallas_call(
        functools.partial(forward_kernel, places),
        out_shape=(jax.ShapeDtypeStruct((2, TILE, TILE), BF),) * 4,
        in_specs=[pl.BlockSpec(memory_space=SMEM)] * 3 + [vmem] * (1 + len(arrays)),
        out_specs=(vmem,) * 4,
        scratch_shapes=[VMEM((2 * NX * NZ * NY, TILE, TILE), BF)],
        compiler_params=pltpu.CompilerParams(vmem_limit_bytes=24 * 2**20),
        cost_estimate=pl.CostEstimate(flops=2 * rows * slots * TILE**3, bytes_accessed=11 * 2**20, transcendentals=0),
        name="forward",
    )(rep, counts, positions, edge_tiles, *arrays)


def middle_kernel(rep_ref, p0, p1, p2, p3, weight_ref, bias_ref, cot_ref, hidden_ref, slope_ref, near_ref, pair_ref, far_ref):
    agg = add32(*[jnp.concatenate([p[0], p[1]], axis=0) for p in (p0, p1, p2, p3)])
    weight = weight_ref[...]
    preact = (
        jnp.dot(agg, weight.astype(F32), preferred_element_type=F32, precision=lax.Precision.HIGHEST)
        + bias_ref[...]
    )
    gate = jax.nn.sigmoid(preact)
    hidden_ref[...] = (preact * gate).astype(BF)
    outgrad = (cot_ref[...].astype(F32) * gate * (1.0 + preact * (1.0 - gate))).astype(BF)
    slope = lax.dot_general(weight, outgrad, (((1,), (1,)), ((), ())), preferred_element_type=F32).astype(BF)
    for i in range(slope_ref.shape[0]):
        slope_ref[i] = slope[:, i * TILE:(i + 1) * TILE]
    wide = outgrad.astype(F32)
    grad = lax.dot_general(
        agg, wide, (((0,), (0,)), ((), ())), preferred_element_type=F32, precision=lax.Precision.HIGHEST
    )
    bias = jnp.sum(wide, axis=0, keepdims=True)
    places = (near_ref, (pair_ref, 0), far_ref, (pair_ref, 1))
    for q in range(4):
        if q % 2:
            ref = places[q][0].at[places[q][1]]
        else:
            ref = places[q]
        for p in range(4):

            @pl.when(rep_ref[0] ^ q == p)
            def _(ref=ref, p=p):
                ref[0:32, :] = grad[p * 32:(p + 1) * 32, 0:TILE]
                ref[32:64, :] = grad[p * 32:(p + 1) * 32, TILE:]

        ref[64:72, :] = jnp.broadcast_to(bias[:, 0:TILE], (8, TILE))
        ref[72:80, :] = jnp.broadcast_to(bias[:, TILE:], (8, TILE))


def middle(rep, parts, weight, bias, cotangent):
    nodes, width = cotangent.shape
    vmem = pl.BlockSpec(memory_space=VMEM)
    quarter = jax.ShapeDtypeStruct((80, TILE), F32)
    return pl.pallas_call(
        middle_kernel,
        out_shape=(
            jax.ShapeDtypeStruct((nodes, width), BF),
            jax.ShapeDtypeStruct((nodes // TILE, TILE, TILE), BF),
            quarter,
            jax.ShapeDtypeStruct((2, 80, TILE), F32),
            quarter,
        ),
        in_specs=[pl.BlockSpec(memory_space=SMEM)] + [vmem] * 7,
        out_specs=(vmem,) * 5,
        compiler_params=pltpu.CompilerParams(vmem_limit_bytes=32 * 2**20),
        name="middle",
    )(rep, *parts, weight, bias.reshape(1, -1), cotangent)


def backward_kernel(places, count_ref, pos_ref, edges, slope_ref, *rest):
    outs, totals = rest[:-1], rest[-1]
    slots = edges.shape[2]

    def clear(i, carry):
        totals[pl.ds(i * 8, 8)] = jnp.zeros((8, TILE, TILE), F32)
        return carry

    lax.fori_loop(0, totals.shape[0] // 8, clear, 0)

    def body(t, count, size):
        slope = slope_ref[t]
        for g in range(size // GROUP):
            which = range(g * GROUP, (g + 1) * GROUP)
            tiles = [live_tile(edges, t, s, count) for s in which]
            terms = jnp.dot(slope, jnp.concatenate(tiles, axis=1), preferred_element_type=F32)
            where = [pos_ref[t * slots + s] for s in which]
            old = [totals[w] for w in where]
            for i, w in enumerate(where):
                totals[w] = old[i] + terms[:, i * TILE:(i + 1) * TILE]

    each_row(count_ref, edges, body)

    for out, (place, size) in zip(outs, places):

        def store(i, carry, out=out, place=place):
            out[pl.ds(i * 4, 4)] = totals[pl.ds(place + i * 4, 4)].astype(out.dtype)
            return carry

        lax.fori_loop(0, size // 4, store, 0)


def backward(counts, positions, edge_tiles, slope, places):
    rows, _, slots = edge_tiles.shape[:3]
    vmem = pl.BlockSpec(memory_space=VMEM)
    return pl.pallas_call(
        functools.partial(backward_kernel, places),
        out_shape=tuple(jax.ShapeDtypeStruct((size, TILE, TILE), BF) for _, size in places),
        in_specs=[pl.BlockSpec(memory_space=SMEM)] * 2 + [vmem, vmem],
        out_specs=(vmem,) * len(places),
        scratch_shapes=[VMEM((2 * NX * NZ * NY, TILE, TILE), F32)],
        compiler_params=pltpu.CompilerParams(vmem_limit_bytes=28 * 2**20),
        cost_estimate=pl.CostEstimate(flops=2 * rows * slots * TILE**3, bytes_accessed=15 * 2**20, transcendentals=0),
        name="backward",
    )(counts, positions, edge_tiles, slope)


def last_kernel(own_ref, got_ref, quarter_ref, feature_ref, weight_ref, bias_ref):
    for i in range(2):
        total = own_ref[i] + got_ref[i].astype(F32)
        feature_ref[0, i * TILE:(i + 1) * TILE, :] = total.T.astype(BF)
    for q in range(4):
        weight_ref[q * 32:(q + 1) * 32, 0:TILE] = quarter_ref[q, 0:32, :]
        weight_ref[q * 32:(q + 1) * 32, TILE:] = quarter_ref[q, 32:64, :]
    bias_ref[:, 0:TILE] = quarter_ref[0, 64:65, :]
    bias_ref[:, TILE:] = quarter_ref[0, 72:73, :]


def last(own, got, quarters):
    vmem = pl.BlockSpec(memory_space=VMEM)
    return pl.pallas_call(
        last_kernel,
        out_shape=(
            jax.ShapeDtypeStruct((1, 2 * TILE, TILE), BF),
            jax.ShapeDtypeStruct((TILE, 2 * TILE), F32),
            jax.ShapeDtypeStruct((1, 2 * TILE), F32),
        ),
        in_specs=[vmem] * 3,
        out_specs=(vmem, vmem, vmem),
        name="last",
    )(own, got, quarters)


def gather_features(own):
    other = swap(own, "y")
    plane = jnp.concatenate([own, shift_x(own, 1), shift_x(own, 2), shift_x(own, -1)])
    spread = jnp.broadcast_to(other[None], (NZ,) + other.shape).reshape(2 * NZ, TILE, TILE)
    line = lax.all_to_all(spread, "z", 0, 0, tiled=True)
    pieces = [(0, plane), (64, line)]
    for k, hop in ((1, 1), (2, 2), (3, -1)):
        pieces.append((64 + 16 * k, shift_x(line, hop)))
    up = down = plane
    for k in (1, 2, 3):
        up, down = shift_z(up, 1), shift_z(down, -1)
        pieces += [(8 * k, up), (8 * (8 - k), down)]
    pieces += [(32, shift_z(up[:4], 1)), (36, shift_z(down[4:], -1))]
    return pieces


A_PLACES = ((32, 4), (36, 4)) + tuple((8 * k, 8) for k in (3, 5, 2, 6, 1, 7, 0))
B_PLACES = tuple((64 + 16 * k, 16) for k in range(4))


def split(value):
    high = lax.reduce_precision(value, 8, 7)
    return jnp.concatenate([high.astype(BF), (value - high).astype(BF)])


def join(value):
    half = value.shape[0] // 2
    return value[:half].astype(F32) + value[half:].astype(F32)


def scatter_totals(parts, grad):
    rows = [p.reshape(-1, TILE) for p in parts]
    up, down = rows[0], rows[1]
    ups, downs = [None, rows[2], rows[4], rows[6]], [None, rows[3], rows[5], rows[7]]
    b = rows[9:]
    line = add(b[0], shift_x(b[1], 1), shift_x(b[2], 2), shift_x(b[3], -1))
    half, full = 4 * TILE, 8 * TILE
    wide = split(grad)
    grads = [grad]
    ride_up = ride_down = wide
    for step in range(4):
        if step == 2:
            up, line = lax.optimization_barrier((up, line))
        up = shift_z(jnp.concatenate([up, ride_up]), 1)
        if step < 3:
            down = shift_z(jnp.concatenate([down, ride_down]), -1)
            size = half if step == 0 else full
            ride_up, ride_down = up[size:], down[size:]
            grads += [join(ride_up), join(ride_down)]
            up, down = up[:size], down[:size]
            if step == 0:
                up = jnp.concatenate([add(up, ups[1][:half]), ups[1][half:]])
                down = jnp.concatenate([downs[1][:half], add(down, downs[1][half:])])
            else:
                up, down = add(up, ups[step + 1]), add(down, downs[step + 1])
        else:
            down = shift_z(down, -1)
            grads.append(join(up[full:]))
            up = up[:full]
    line = lax.all_to_all(line.reshape(2 * NZ, TILE, TILE), "z", 0, 0, tiled=True)
    theirs = swap(add(*[line[2 * k:2 * k + 2] for k in range(NZ)]), "y")
    grad = add32(*grads)
    wide = split(grad)
    part = 2 * TILE
    total = add32(rows[8], up, down)
    sent = [total[k * part:(k + 1) * part].astype(BF) for k in (1, 2, 3)]
    got = [shift_x(jnp.concatenate([v, wide]), hop) for v, hop in zip(sent, (1, 2, -1))]
    total = add32(total[:part], *[g[:part] for g in got])
    grad = add32(grad, *[join(g[part:]) for g in got])
    return total.reshape(2, TILE, TILE), theirs, grad


def shards(features, weight, bias_vector, edge_tiles, tile_columns, live_counts, cotangent):
    x, z, y = lax.axis_index("x"), lax.axis_index("z"), lax.axis_index("y")
    rep = (lax.axis_index("near") * 2 + lax.axis_index("core")).reshape(1)
    columns = tile_columns.reshape(-1)
    owner, which = columns // 2, columns % 2
    ox, oz, oy = owner // (NZ * NY), (owner // NY) % NZ, owner % NY

    def places(dx, dz):
        return (jnp.where(oy == y, dz * NX + dx, 32 + dx * NZ + oz) * 2 + which).astype(jnp.int32)

    behind = places((x - ox) % NX, (z - oz) % NZ)
    ahead = places((ox - x) % NX, (oz - z) % NZ)
    counts = live_counts.reshape(-1)

    with jax.named_scope("gather"):
        pieces = gather_features(features.reshape(2, TILE, TILE))
    partial = forward(rep, counts, behind, edge_tiles, pieces)
    with jax.named_scope("sections"):
        parts = [
            partial[0],
            swap(partial[1], "core"),
            swap(partial[2], "near"),
            swap(partial[3], "near", "core"),
        ]
    hidden_out, slope, near, pair, far = middle(rep, parts, weight, bias_vector, cotangent)
    with jax.named_scope("weights"):
        pair = swap(pair, "core")
        near, far, slope = lax.optimization_barrier((near + pair[0], far + pair[1], slope))
        grads = [swap(far, "near"), swap(near, "y"), swap(far, "y", "near")]
    with jax.named_scope("slopes"):
        slopes = lax.all_gather(slope, ("near", "core"), axis=0, tiled=True)
        grad = add32(near, *grads)
        slopes, grad = lax.optimization_barrier((slopes, grad))
    totals = backward(counts, ahead, edge_tiles, slopes, A_PLACES + B_PLACES)
    with jax.named_scope("scatter"):
        mine, theirs, grad = scatter_totals(totals, grad)
        quarters = lax.all_gather(grad, ("near", "core"), axis=0)
    feature_grad, weight_grad, bias_grad = last(mine, theirs, quarters)
    return hidden_out, feature_grad, weight_grad, bias_grad.reshape(-1)


def solution(mesh):
    grid = Mesh(mesh.devices.reshape(NX, NZ, NY, 2, 2), ("x", "z", "y", "near", "core"))
    row, rep = ("x", "z", "y"), ("near", "core")
    in_specs = (
        P(rep, row, None),
        P(),
        P(),
        P(row, rep, None, None, None),
        P(row, rep, None),
        P(row, rep),
        P(row + rep, None),
    )
    out_specs = (P(row + rep, None), P(rep, row, None), P(), P())
    return jax.shard_map(shards, mesh=grid, in_specs=in_specs, out_specs=out_specs, check_vma=False)
```

```python
import functools

import jax
import jax.numpy as jnp
from jax import lax
from jax.experimental import pallas as pl
from jax.experimental.pallas import tpu as pltpu
from jax.sharding import Mesh
from jax.sharding import PartitionSpec as P

NX, NZ, NY = 4, 8, 2
TILE = 128
GROUP = 6
BF = jnp.bfloat16
F32 = jnp.float32
VMEM = pltpu.VMEM
SMEM = pltpu.SMEM


def shift_x(value, k):
    return lax.ppermute(value, "x", [(i, (i + k) % NX) for i in range(NX)])


def shift_z(value, k):
    return lax.ppermute(value, "z", [(i, (i + k) % NZ) for i in range(NZ)])


def swap(value, *axes):
    pairs = [(i, (1 << len(axes)) - 1 - i) for i in range(1 << len(axes))]
    return lax.ppermute(value, axes, pairs)


def add32(*values):
    total = values[0].astype(F32)
    for value in values[1:]:
        total = total + value.astype(F32)
    return total


def add(*values):
    return add32(*values).astype(BF)


def each_row(meta_ref, edges, body):
    rows, _, slots = edges.shape[:3]

    def row(t, carry):
        count = meta_ref[t]

        @pl.when(count > GROUP)
        def _():
            body(t, count, slots)

        @pl.when(count <= GROUP)
        def _():
            body(t, count, GROUP)

        return carry

    lax.fori_loop(0, rows, row, 0)


def live_tile(edges, t, s, count):
    tile = edges[t, 0, s]
    return jnp.where(s < count, tile, jnp.zeros_like(tile))


def forward_kernel(places, rep_ref, meta_ref, edges, *rest):
    pieces = rest[: len(places)]
    outs, table = rest[len(places):-1], rest[-1]
    rows, _, slots = edges.shape[:3]
    for piece, (place, size) in zip(pieces, places):

        def copy(i, carry, piece=piece, place=place):
            table[pl.ds(place + i * 4, 4)] = piece[pl.ds(i * 4, 4)]
            return carry

        lax.fori_loop(0, size // 4, copy, 0)

    def body(t, count, size):
        left = [live_tile(edges, t, s, count) for s in range(size)]
        right = [table[meta_ref[rows + t * slots + s]] for s in range(size)]
        total = jnp.dot(
            jnp.concatenate(left, axis=1), jnp.concatenate(right, axis=0), preferred_element_type=F32
        ).astype(BF)
        for q in range(len(outs)):

            @pl.when((t // 2) ^ rep_ref[0] == q)
            def _(q=q):
                outs[q][t % 2] = total

    each_row(meta_ref, edges, body)


def forward(rep, meta, edges, pieces):
    places = tuple((place, piece.shape[0]) for place, piece in pieces)
    arrays = [piece for _, piece in pieces]
    rows, _, slots = edges.shape[:3]
    vmem = pl.BlockSpec(memory_space=VMEM)
    return pl.pallas_call(
        functools.partial(forward_kernel, places),
        out_shape=(jax.ShapeDtypeStruct((2, TILE, TILE), BF),) * 4,
        in_specs=[pl.BlockSpec(memory_space=SMEM)] * 2 + [vmem] * (1 + len(arrays)),
        out_specs=(vmem,) * 4,
        scratch_shapes=[VMEM((2 * NX * NZ * NY, TILE, TILE), BF)],
        compiler_params=pltpu.CompilerParams(vmem_limit_bytes=24 * 2**20),
        cost_estimate=pl.CostEstimate(flops=2 * rows * slots * TILE**3, bytes_accessed=11 * 2**20, transcendentals=0),
        name="forward",
    )(rep, meta, edges, *arrays)


def middle_kernel(rep_ref, p0, p1, p2, p3, weight_ref, bias_ref, cot_ref, hidden_ref, slope_ref, mine_ref, theirs_ref):
    agg = add32(*[jnp.concatenate([p[0], p[1]], axis=0) for p in (p0, p1, p2, p3)])
    weight = weight_ref[...]
    preact = (
        jnp.dot(agg, weight.astype(F32), preferred_element_type=F32, precision=lax.Precision.HIGHEST)
        + bias_ref[...]
    )
    gate = jax.nn.sigmoid(preact)
    hidden_ref[...] = (preact * gate).astype(BF)
    outgrad = (cot_ref[...].astype(F32) * gate * (1.0 + preact * (1.0 - gate))).astype(BF)
    slope = lax.dot_general(weight, outgrad, (((1,), (1,)), ((), ())), preferred_element_type=F32).astype(BF)
    for i in range(slope_ref.shape[0]):
        slope_ref[i] = slope[:, i * TILE:(i + 1) * TILE]
    wide = outgrad.astype(F32)
    grad = lax.dot_general(
        agg, wide, (((0,), (0,)), ((), ())), preferred_element_type=F32, precision=lax.Precision.HIGHEST
    )
    bias = jnp.sum(wide, axis=0, keepdims=True)
    for ref, same in ((mine_ref, True), (theirs_ref, False)):
        for half in range(2):

            @pl.when(((rep_ref[0] % 2) == half) == same)
            def _(ref=ref, half=half):
                ref[0:64, :] = grad[half * 64:(half + 1) * 64, 0:TILE]
                ref[64:128, :] = grad[half * 64:(half + 1) * 64, TILE:]

        ref[128:144, :] = jnp.broadcast_to(bias[:, 0:TILE], (16, TILE))
        ref[144:160, :] = jnp.broadcast_to(bias[:, TILE:], (16, TILE))


def middle(rep, parts, weight, bias, cotangent):
    nodes, width = cotangent.shape
    vmem = pl.BlockSpec(memory_space=VMEM)
    half = jax.ShapeDtypeStruct((160, TILE), F32)
    return pl.pallas_call(
        middle_kernel,
        out_shape=(
            jax.ShapeDtypeStruct((nodes, width), BF),
            jax.ShapeDtypeStruct((nodes // TILE, TILE, TILE), BF),
            half,
            half,
        ),
        in_specs=[pl.BlockSpec(memory_space=SMEM)] + [vmem] * 7,
        out_specs=(vmem,) * 4,
        compiler_params=pltpu.CompilerParams(vmem_limit_bytes=32 * 2**20),
        name="middle",
    )(rep, *parts, weight, bias.reshape(1, -1), cotangent)


def backward_kernel(places, rep_ref, meta_ref, edges, s0, s1, s2, s3, *rest):
    outs, totals, slope_ref = rest[:-2], rest[-2], rest[-1]
    for q, part in enumerate((s0, s1, s2, s3)):
        for i in range(2):
            slope_ref[(rep_ref[0] ^ q) * 2 + i] = part[i]
    rows, _, slots = edges.shape[:3]

    def clear(i, carry):
        totals[pl.ds(i * 8, 8)] = jnp.zeros((8, TILE, TILE), F32)
        return carry

    lax.fori_loop(0, totals.shape[0] // 8, clear, 0)

    def body(t, count, size):
        slope = slope_ref[t]
        for g in range(size // GROUP):
            which = range(g * GROUP, (g + 1) * GROUP)
            tiles = [live_tile(edges, t, s, count) for s in which]
            terms = jnp.dot(slope, jnp.concatenate(tiles, axis=1), preferred_element_type=F32)
            where = [meta_ref[rows + t * slots + s] for s in which]
            old = [totals[w] for w in where]
            for i, w in enumerate(where):
                totals[w] = old[i] + terms[:, i * TILE:(i + 1) * TILE]

    each_row(meta_ref, edges, body)

    for out, segments in zip(outs, places):
        offset = 0
        for place, size in segments:

            def store(i, carry, out=out, place=place, offset=offset):
                out[pl.ds(offset + i * 4, 4)] = totals[pl.ds(place + i * 4, 4)].astype(out.dtype)
                return carry

            lax.fori_loop(0, size // 4, store, 0)
            offset += size


def backward(rep, meta, edges, slopes, places):
    rows, _, slots = edges.shape[:3]
    vmem = pl.BlockSpec(memory_space=VMEM)
    return pl.pallas_call(
        functools.partial(backward_kernel, places),
        out_shape=tuple(
            jax.ShapeDtypeStruct((sum(size for _, size in segments), TILE, TILE), BF) for segments in places
        ),
        in_specs=[pl.BlockSpec(memory_space=SMEM)] * 2 + [vmem] * 5,
        out_specs=(vmem,) * len(places),
        scratch_shapes=[VMEM((2 * NX * NZ * NY, TILE, TILE), F32), VMEM((rows, TILE, TILE), BF)],
        compiler_params=pltpu.CompilerParams(vmem_limit_bytes=28 * 2**20),
        cost_estimate=pl.CostEstimate(flops=2 * rows * slots * TILE**3, bytes_accessed=15 * 2**20, transcendentals=0),
        name="backward",
    )(rep, meta, edges, *slopes)


def last_kernel(rep_ref, total_ref, mine_ref, theirs_ref, feature_ref, weight_ref, bias_ref):
    for i in range(2):
        feature_ref[0, i * TILE:(i + 1) * TILE, :] = total_ref[i].T.astype(BF)
    for ref, same in ((mine_ref, True), (theirs_ref, False)):
        for half in range(2):

            @pl.when(((rep_ref[0] % 2) == half) == same)
            def _(ref=ref, half=half):
                weight_ref[half * 64:(half + 1) * 64, 0:TILE] = ref[0:64, :]
                weight_ref[half * 64:(half + 1) * 64, TILE:] = ref[64:128, :]
                if half == 0:
                    bias_ref[:, 0:TILE] = ref[128:129, :]
                    bias_ref[:, TILE:] = ref[144:145, :]


def last(rep, total, mine, theirs):
    vmem = pl.BlockSpec(memory_space=VMEM)
    return pl.pallas_call(
        last_kernel,
        out_shape=(
            jax.ShapeDtypeStruct((1, 2 * TILE, TILE), BF),
            jax.ShapeDtypeStruct((TILE, 2 * TILE), F32),
            jax.ShapeDtypeStruct((1, 2 * TILE), F32),
        ),
        in_specs=[pl.BlockSpec(memory_space=SMEM)] + [vmem] * 3,
        out_specs=(vmem, vmem, vmem),
        name="last",
    )(rep, total, mine, theirs)


def gather_features(own):
    own, other = lax.optimization_barrier((own, swap(own, "y")))
    plane = jnp.concatenate([own, shift_x(own, 1), shift_x(own, 2), shift_x(own, -1)])
    spread = jnp.broadcast_to(other[None], (NZ,) + other.shape).reshape(2 * NZ, TILE, TILE)
    line = lax.all_to_all(spread, "z", 0, 0, tiled=True)
    pieces = [(0, plane), (64, line)]
    ahead, behind = shift_x(line, 1), shift_x(line, -1)
    up = down = plane
    for k in (1, 2, 3):
        up, down = shift_z(up, 1), shift_z(down, -1)
        pieces += [(8 * k, up), (8 * (8 - k), down)]
        if k == 2:
            up, ahead, behind = lax.optimization_barrier((up, ahead, behind))
    pieces += [(80, ahead), (112, behind), (96, shift_x(ahead[:8], 1)), (104, shift_x(behind[8:], -1))]
    pieces += [(32, shift_z(up[:4], 1)), (36, shift_z(down[4:], -1))]
    return pieces


OWN_PLACES = tuple(((8 * k, 8),) for k in (4, 3, 5, 2, 6, 1, 7, 0))
OTHER_PLACES = tuple(tuple((64 + 8 * k, 8) for k in ks) for ks in ((4,), (3, 5), (2, 6), (1, 7), (0,)))


def scatter_totals(parts, grad):
    rows = [p.reshape(-1, TILE) for p in parts]
    own, other = rows[:8], rows[8:]
    half, full = 4 * TILE, 8 * TILE
    first = swap(jnp.concatenate([other[0], grad.astype(BF)]), "y")
    wide = add(grad, first[full:])
    last = add(own[0], first[:full])
    up, down = last[:half], last[half:]
    ride_up = ride_down = wide
    grads = [wide]
    for step in range(4):
        moved_up = shift_z(jnp.concatenate([up, ride_up]), 1)
        moved_down = shift_z(down if step == 3 else jnp.concatenate([down, ride_down]), -1)
        met = swap(other[step + 1], "y")
        up, down, met = lax.optimization_barrier((moved_up, moved_down, met))
        size = half if step == 0 else full
        ride_up, ride_down = up[size:], down[size:]
        grads.append(ride_up)
        if step < 3:
            grads.append(ride_down)
        up, down = up[:size], down[:size]
        if step == 3:
            total = add32(own[7], met, up, down)
            break
        here_up, here_down = add32(own[2 * step + 1], met[:full]), add32(own[2 * step + 2], met[full:])
        if step == 0:
            up = jnp.concatenate([add(here_up[:half], up), here_up[half:].astype(BF)])
            down = jnp.concatenate([here_down[:half].astype(BF), add(here_down[half:], down)])
        else:
            up, down = add(here_up, up), add(here_down, down)
    wide = add(*grads)
    part = 2 * TILE
    sent = [total[k * part:(k + 1) * part].astype(BF) for k in (1, 2, 3)]
    got = [shift_x(jnp.concatenate([v, wide]), hop) for v, hop in zip(sent, (1, 2, -1))]
    total = add32(total[:part], *[g[:part] for g in got])
    grad = add32(wide, *[g[part:] for g in got])
    return total.reshape(2, TILE, TILE), grad


def shards(features, weight, bias_vector, edge_tiles, tile_columns, live_counts, cotangent):
    x, z, y = lax.axis_index("x"), lax.axis_index("z"), lax.axis_index("y")
    rep = (lax.axis_index("near") * 2 + lax.axis_index("core")).reshape(1)
    columns = tile_columns.reshape(-1)
    owner, which = columns // 2, columns % 2
    ox, oz, oy = owner // (NZ * NY), (owner // NY) % NZ, owner % NY

    def places(dx, dz, elsewhere):
        return (jnp.where(oy == y, dz * NX + dx, 32 + elsewhere) * 2 + which).astype(jnp.int32)

    counts = live_counts.reshape(-1)
    behind = jnp.concatenate([counts, places((x - ox) % NX, (z - oz) % NZ, (x - ox) % NX * NZ + oz)])
    ahead = jnp.concatenate([counts, places((ox - x) % NX, (oz - z) % NZ, (oz - z) % NZ * NX + (ox - x) % NX)])

    with jax.named_scope("gather"):
        pieces = gather_features(features.reshape(2, TILE, TILE))
    partial = forward(rep, behind, edge_tiles, pieces)
    with jax.named_scope("sections"):
        parts = [
            partial[0],
            swap(partial[1], "core"),
            swap(partial[2], "near"),
            swap(partial[3], "near", "core"),
        ]
    hidden_out, slope, mine, theirs = middle(rep, parts, weight, bias_vector, cotangent)
    with jax.named_scope("slopes"):
        slopes = [slope, swap(slope, "core"), swap(slope, "near"), swap(slope, "near", "core")]
    with jax.named_scope("weights"):
        mine = mine + swap(theirs, "core")
        grad = mine + swap(mine, "near")
    totals = backward(rep, ahead, edge_tiles, slopes, OWN_PLACES + OTHER_PLACES)
    with jax.named_scope("scatter"):
        total, grad = scatter_totals(totals, grad)
        halves = [grad, swap(grad, "core")]
    feature_grad, weight_grad, bias_grad = last(rep, total, *halves)
    return hidden_out, feature_grad, weight_grad, bias_grad.reshape(-1)


def solution(mesh):
    grid = Mesh(mesh.devices.reshape(NX, NZ, NY, 2, 2), ("x", "z", "y", "near", "core"))
    row, rep = ("x", "z", "y"), ("near", "core")
    in_specs = (
        P(rep, row, None),
        P(),
        P(),
        P(row, rep, None, None, None),
        P(row, rep, None),
        P(row, rep),
        P(row + rep, None),
    )
    out_specs = (P(row + rep, None), P(rep, row, None), P(), P())
    return jax.shard_map(shards, mesh=grid, in_specs=in_specs, out_specs=out_specs, check_vma=False)
```

```python
import functools

import jax
import jax.numpy as jnp
from jax import lax
from jax.experimental import pallas as pl
from jax.experimental.pallas import tpu as pltpu
from jax.sharding import Mesh
from jax.sharding import PartitionSpec as P

NX, NZ, NY = 4, 8, 2
TILE = 128
GROUP = 6
BF = jnp.bfloat16
F32 = jnp.float32
VMEM = pltpu.VMEM
SMEM = pltpu.SMEM


def shift_x(value, k):
    return lax.ppermute(value, "x", [(i, (i + k) % NX) for i in range(NX)])


def shift_z(value, k):
    return lax.ppermute(value, "z", [(i, (i + k) % NZ) for i in range(NZ)])


def swap(value, *axes):
    pairs = [(i, (1 << len(axes)) - 1 - i) for i in range(1 << len(axes))]
    return lax.ppermute(value, axes, pairs)


def add32(*values):
    total = values[0].astype(F32)
    for value in values[1:]:
        total = total + value.astype(F32)
    return total


def add(*values):
    return add32(*values).astype(BF)


def each_row(meta_ref, edges, body):
    rows, _, slots = edges.shape[:3]

    def row(t, carry):
        count = meta_ref[t]

        @pl.when(count > GROUP)
        def _():
            body(t, count, slots)

        @pl.when(count <= GROUP)
        def _():
            body(t, count, GROUP)

        return carry

    lax.fori_loop(0, rows, row, 0)


def live_tile(edges, t, s, count):
    tile = edges[t, 0, s]
    return jnp.where(s < count, tile, jnp.zeros_like(tile))


def forward_kernel(places, rep_ref, meta_ref, edges, *rest):
    pieces = rest[: len(places)]
    outs, table = rest[len(places):-1], rest[-1]
    rows, _, slots = edges.shape[:3]
    for piece, (place, size) in zip(pieces, places):

        def copy(i, carry, piece=piece, place=place):
            table[pl.ds(place + i * 4, 4)] = piece[pl.ds(i * 4, 4)]
            return carry

        lax.fori_loop(0, size // 4, copy, 0)

    def body(t, count, size):
        left = [live_tile(edges, t, s, count) for s in range(size)]
        right = [table[meta_ref[rows + t * slots + s]] for s in range(size)]
        total = jnp.dot(
            jnp.concatenate(left, axis=1), jnp.concatenate(right, axis=0), preferred_element_type=F32
        ).astype(BF)
        for q in range(len(outs)):

            @pl.when((t // 2) ^ rep_ref[0] == q)
            def _(q=q):
                outs[q][t % 2] = total

    each_row(meta_ref, edges, body)


def forward(rep, meta, edges, pieces):
    places = tuple((place, piece.shape[0]) for place, piece in pieces)
    arrays = [piece for _, piece in pieces]
    rows, _, slots = edges.shape[:3]
    vmem = pl.BlockSpec(memory_space=VMEM)
    return pl.pallas_call(
        functools.partial(forward_kernel, places),
        out_shape=(jax.ShapeDtypeStruct((2, TILE, TILE), BF),) * 4,
        in_specs=[pl.BlockSpec(memory_space=SMEM)] * 2 + [vmem] * (1 + len(arrays)),
        out_specs=(vmem,) * 4,
        scratch_shapes=[VMEM((2 * NX * NZ * NY, TILE, TILE), BF)],
        compiler_params=pltpu.CompilerParams(vmem_limit_bytes=24 * 2**20),
        cost_estimate=pl.CostEstimate(flops=2 * rows * slots * TILE**3, bytes_accessed=11 * 2**20, transcendentals=0),
        name="forward",
    )(rep, meta, edges, *arrays)


def middle_kernel(rep_ref, p0, p1, p2, p3, weight_ref, bias_ref, cot_ref, hidden_ref, slope_ref, mine_ref, theirs_ref):
    agg = add32(*[jnp.concatenate([p[0], p[1]], axis=0) for p in (p0, p1, p2, p3)])
    weight = weight_ref[...]
    preact = (
        jnp.dot(agg, weight.astype(F32), preferred_element_type=F32, precision=lax.Precision.HIGHEST)
        + bias_ref[...]
    )
    gate = jax.nn.sigmoid(preact)
    hidden_ref[...] = (preact * gate).astype(BF)
    outgrad = (cot_ref[...].astype(F32) * gate * (1.0 + preact * (1.0 - gate))).astype(BF)
    slope = lax.dot_general(weight, outgrad, (((1,), (1,)), ((), ())), preferred_element_type=F32).astype(BF)
    for i in range(slope_ref.shape[0]):
        slope_ref[i] = slope[:, i * TILE:(i + 1) * TILE]
    wide = outgrad.astype(F32)
    grad = lax.dot_general(
        agg, wide, (((0,), (0,)), ((), ())), preferred_element_type=F32, precision=lax.Precision.HIGHEST
    )
    bias = jnp.sum(wide, axis=0, keepdims=True)
    for ref, same in ((mine_ref, True), (theirs_ref, False)):
        for half in range(2):

            @pl.when(((rep_ref[0] % 2) == half) == same)
            def _(ref=ref, half=half):
                ref[0:64, :] = grad[half * 64:(half + 1) * 64, 0:TILE]
                ref[64:128, :] = grad[half * 64:(half + 1) * 64, TILE:]

        ref[128:144, :] = jnp.broadcast_to(bias[:, 0:TILE], (16, TILE))
        ref[144:160, :] = jnp.broadcast_to(bias[:, TILE:], (16, TILE))


def middle(rep, parts, weight, bias, cotangent):
    nodes, width = cotangent.shape
    vmem = pl.BlockSpec(memory_space=VMEM)
    half = jax.ShapeDtypeStruct((160, TILE), F32)
    return pl.pallas_call(
        middle_kernel,
        out_shape=(
            jax.ShapeDtypeStruct((nodes, width), BF),
            jax.ShapeDtypeStruct((nodes // TILE, TILE, TILE), BF),
            half,
            half,
        ),
        in_specs=[pl.BlockSpec(memory_space=SMEM)] + [vmem] * 7,
        out_specs=(vmem,) * 4,
        compiler_params=pltpu.CompilerParams(vmem_limit_bytes=32 * 2**20),
        name="middle",
    )(rep, *parts, weight, bias.reshape(1, -1), cotangent)


def backward_kernel(places, rep_ref, meta_ref, edges, s0, s1, s2, s3, *rest):
    outs, totals, slope_ref = rest[:-2], rest[-2], rest[-1]
    for q, part in enumerate((s0, s1, s2, s3)):
        for i in range(2):
            slope_ref[(rep_ref[0] ^ q) * 2 + i] = part[i]
    rows, _, slots = edges.shape[:3]

    def clear(i, carry):
        totals[pl.ds(i * 8, 8)] = jnp.zeros((8, TILE, TILE), F32)
        return carry

    lax.fori_loop(0, totals.shape[0] // 8, clear, 0)

    def body(t, count, size):
        slope = slope_ref[t]
        for g in range(size // GROUP):
            which = range(g * GROUP, (g + 1) * GROUP)
            tiles = [live_tile(edges, t, s, count) for s in which]
            terms = jnp.dot(slope, jnp.concatenate(tiles, axis=1), preferred_element_type=F32)
            where = [meta_ref[rows + t * slots + s] for s in which]
            old = [totals[w] for w in where]
            for i, w in enumerate(where):
                totals[w] = old[i] + terms[:, i * TILE:(i + 1) * TILE]

    each_row(meta_ref, edges, body)

    for out, segments in zip(outs, places):
        offset = 0
        for place, size in segments:

            def store(i, carry, out=out, place=place, offset=offset):
                out[pl.ds(offset + i * 4, 4)] = totals[pl.ds(place + i * 4, 4)].astype(out.dtype)
                return carry

            lax.fori_loop(0, size // 4, store, 0)
            offset += size


def backward(rep, meta, edges, slopes, places):
    rows, _, slots = edges.shape[:3]
    vmem = pl.BlockSpec(memory_space=VMEM)
    return pl.pallas_call(
        functools.partial(backward_kernel, places),
        out_shape=tuple(
            jax.ShapeDtypeStruct((sum(size for _, size in segments), TILE, TILE), BF) for segments in places
        ),
        in_specs=[pl.BlockSpec(memory_space=SMEM)] * 2 + [vmem] * 5,
        out_specs=(vmem,) * len(places),
        scratch_shapes=[VMEM((2 * NX * NZ * NY, TILE, TILE), F32), VMEM((rows, TILE, TILE), BF)],
        compiler_params=pltpu.CompilerParams(vmem_limit_bytes=28 * 2**20),
        cost_estimate=pl.CostEstimate(flops=2 * rows * slots * TILE**3, bytes_accessed=15 * 2**20, transcendentals=0),
        name="backward",
    )(rep, meta, edges, *slopes)


def last_kernel(rep_ref, total_ref, mine_ref, theirs_ref, feature_ref, weight_ref, bias_ref):
    for i in range(2):
        feature_ref[0, i * TILE:(i + 1) * TILE, :] = total_ref[i].T.astype(BF)
    for ref, same in ((mine_ref, True), (theirs_ref, False)):
        for half in range(2):

            @pl.when(((rep_ref[0] % 2) == half) == same)
            def _(ref=ref, half=half):
                weight_ref[half * 64:(half + 1) * 64, 0:TILE] = ref[0:64, :]
                weight_ref[half * 64:(half + 1) * 64, TILE:] = ref[64:128, :]
                if half == 0:
                    bias_ref[:, 0:TILE] = ref[128:129, :]
                    bias_ref[:, TILE:] = ref[144:145, :]


def last(rep, total, mine, theirs):
    vmem = pl.BlockSpec(memory_space=VMEM)
    return pl.pallas_call(
        last_kernel,
        out_shape=(
            jax.ShapeDtypeStruct((1, 2 * TILE, TILE), BF),
            jax.ShapeDtypeStruct((TILE, 2 * TILE), F32),
            jax.ShapeDtypeStruct((1, 2 * TILE), F32),
        ),
        in_specs=[pl.BlockSpec(memory_space=SMEM)] + [vmem] * 3,
        out_specs=(vmem, vmem, vmem),
        name="last",
    )(rep, total, mine, theirs)


def gather_features(own):
    own, other = lax.optimization_barrier((own, swap(own, "y")))
    plane = jnp.concatenate([own, shift_x(own, 1), shift_x(own, 2), shift_x(own, -1)])
    spread = jnp.broadcast_to(other[None], (NZ,) + other.shape).reshape(2 * NZ, TILE, TILE)
    line = lax.all_to_all(spread, "z", 0, 0, tiled=True)
    pieces = [(0, plane), (64, line)]
    ahead, behind = shift_x(line, 1), shift_x(line, -1)
    up = down = plane
    for k in (1, 2, 3):
        up, down = shift_z(up, 1), shift_z(down, -1)
        pieces += [(8 * k, up), (8 * (8 - k), down)]
        if k == 2:
            up, ahead, behind = lax.optimization_barrier((up, ahead, behind))
    pieces += [(80, ahead), (112, behind), (96, shift_x(ahead, 1))]
    pieces += [(32, shift_z(up[:4], 1)), (36, shift_z(down[4:], -1))]
    return pieces


OWN_PLACES = tuple(((8 * k, 8),) for k in (4, 3, 5, 2, 6, 1, 7, 0))
OTHER_PLACES = tuple(tuple((64 + 8 * k, 8) for k in ks) for ks in ((4,), (3, 5), (2, 6), (1, 7), (0,)))


def scatter_totals(parts, grad):
    rows = [p.reshape(-1, TILE) for p in parts]
    own, other = rows[:8], rows[8:]
    half, full = 4 * TILE, 8 * TILE
    first = swap(jnp.concatenate([other[0], grad.astype(BF)]), "y")
    wide = add(grad, first[full:])
    last = add(own[0], first[:full])
    up, down = last[:half], last[half:]
    ride_up = ride_down = wide
    grads = [wide]
    for step in range(4):
        moved_up = shift_z(jnp.concatenate([up, ride_up]), 1)
        moved_down = shift_z(down if step == 3 else jnp.concatenate([down, ride_down]), -1)
        met = swap(other[step + 1], "y")
        up, down, met = lax.optimization_barrier((moved_up, moved_down, met))
        size = half if step == 0 else full
        ride_up, ride_down = up[size:], down[size:]
        grads.append(ride_up)
        if step < 3:
            grads.append(ride_down)
        up, down = up[:size], down[:size]
        if step == 3:
            total = add32(own[7], met, up, down)
            break
        here_up, here_down = add32(own[2 * step + 1], met[:full]), add32(own[2 * step + 2], met[full:])
        if step == 0:
            up = jnp.concatenate([add(here_up[:half], up), here_up[half:].astype(BF)])
            down = jnp.concatenate([here_down[:half].astype(BF), add(here_down[half:], down)])
        else:
            up, down = add(here_up, up), add(here_down, down)
    wide = add(*grads)
    part = 2 * TILE
    sent = [total[k * part:(k + 1) * part].astype(BF) for k in (1, 2, 3)]
    got = [shift_x(jnp.concatenate([v, wide]), hop) for v, hop in zip(sent, (1, 2, -1))]
    total = add32(total[:part], *[g[:part] for g in got])
    grad = add32(wide, *[g[part:] for g in got])
    return total.reshape(2, TILE, TILE), grad


def shards(features, weight, bias_vector, edge_tiles, tile_columns, live_counts, cotangent):
    x, z, y = lax.axis_index("x"), lax.axis_index("z"), lax.axis_index("y")
    rep = (lax.axis_index("near") * 2 + lax.axis_index("core")).reshape(1)
    columns = tile_columns.reshape(-1)
    owner, which = columns // 2, columns % 2
    ox, oz, oy = owner // (NZ * NY), (owner // NY) % NZ, owner % NY

    def places(dx, dz, elsewhere):
        return (jnp.where(oy == y, dz * NX + dx, 32 + elsewhere) * 2 + which).astype(jnp.int32)

    counts = live_counts.reshape(-1)
    behind = jnp.concatenate([counts, places((x - ox) % NX, (z - oz) % NZ, (x - ox) % NX * NZ + oz)])
    ahead = jnp.concatenate([counts, places((ox - x) % NX, (oz - z) % NZ, (oz - z) % NZ * NX + (ox - x) % NX)])

    with jax.named_scope("gather"):
        pieces = gather_features(features.reshape(2, TILE, TILE))
    partial = forward(rep, behind, edge_tiles, pieces)
    with jax.named_scope("sections"):
        parts = [
            partial[0],
            swap(partial[1], "core"),
            swap(partial[2], "near"),
            swap(partial[3], "near", "core"),
        ]
    hidden_out, slope, mine, theirs = middle(rep, parts, weight, bias_vector, cotangent)
    with jax.named_scope("slopes"):
        slopes = [slope, swap(slope, "core"), swap(slope, "near"), swap(slope, "near", "core")]
    with jax.named_scope("weights"):
        mine = mine + swap(theirs, "core")
        grad = mine + swap(mine, "near")
    totals = backward(rep, ahead, edge_tiles, slopes, OWN_PLACES + OTHER_PLACES)
    with jax.named_scope("scatter"):
        total, grad = scatter_totals(totals, grad)
        halves = [grad, swap(grad, "core")]
    feature_grad, weight_grad, bias_grad = last(rep, total, *halves)
    return hidden_out, feature_grad, weight_grad, bias_grad.reshape(-1)


def solution(mesh):
    grid = Mesh(mesh.devices.reshape(NX, NZ, NY, 2, 2), ("x", "z", "y", "near", "core"))
    row, rep = ("x", "z", "y"), ("near", "core")
    in_specs = (
        P(rep, row, None),
        P(),
        P(),
        P(row, rep, None, None, None),
        P(row, rep, None),
        P(row, rep),
        P(row + rep, None),
    )
    out_specs = (P(row + rep, None), P(rep, row, None), P(), P())
    return jax.shard_map(shards, mesh=grid, in_specs=in_specs, out_specs=out_specs, check_vma=False)
```

```python
import functools

import jax
import jax.numpy as jnp
from jax import lax
from jax.experimental import pallas as pl
from jax.experimental.pallas import tpu as pltpu
from jax.sharding import Mesh
from jax.sharding import PartitionSpec as P

NX, NZ, NY = 4, 8, 2
TILE = 128
GROUP = 6
BF = jnp.bfloat16
F32 = jnp.float32
VMEM = pltpu.VMEM
SMEM = pltpu.SMEM


def shift_x(value, k):
    return lax.ppermute(value, "x", [(i, (i + k) % NX) for i in range(NX)])


def shift_z(value, k):
    return lax.ppermute(value, "z", [(i, (i + k) % NZ) for i in range(NZ)])


def swap(value, *axes):
    pairs = [(i, (1 << len(axes)) - 1 - i) for i in range(1 << len(axes))]
    return lax.ppermute(value, axes, pairs)


def add32(*values):
    total = values[0].astype(F32)
    for value in values[1:]:
        total = total + value.astype(F32)
    return total


def add(*values):
    return add32(*values).astype(BF)


def each_row(meta_ref, edges, body):
    rows, _, slots = edges.shape[:3]

    def row(t, carry):
        count = meta_ref[t]

        @pl.when(count > GROUP)
        def _():
            body(t, count, slots)

        @pl.when(count <= GROUP)
        def _():
            body(t, count, GROUP)

        return carry

    lax.fori_loop(0, rows, row, 0)


def live_tile(edges, t, s, count):
    tile = edges[t, 0, s]
    return jnp.where(s < count, tile, jnp.zeros_like(tile))


def forward_kernel(places, rep_ref, meta_ref, edges, *rest):
    pieces = rest[: len(places)]
    outs, table = rest[len(places):-1], rest[-1]
    rows, _, slots = edges.shape[:3]
    for piece, (place, size) in zip(pieces, places):

        def copy(i, carry, piece=piece, place=place):
            table[pl.ds(place + i * 4, 4)] = piece[pl.ds(i * 4, 4)]
            return carry

        lax.fori_loop(0, size // 4, copy, 0)

    def body(t, count, size):
        left = [live_tile(edges, t, s, count) for s in range(size)]
        right = [table[meta_ref[rows + t * slots + s]] for s in range(size)]
        total = jnp.dot(
            jnp.concatenate(left, axis=1), jnp.concatenate(right, axis=0), preferred_element_type=F32
        ).astype(BF)
        for q in range(len(outs)):

            @pl.when((t // 2) ^ rep_ref[0] == q)
            def _(q=q):
                outs[q][t % 2] = total

    each_row(meta_ref, edges, body)


def forward(rep, meta, edges, pieces):
    places = tuple((place, piece.shape[0]) for place, piece in pieces)
    arrays = [piece for _, piece in pieces]
    rows, _, slots = edges.shape[:3]
    vmem = pl.BlockSpec(memory_space=VMEM)
    return pl.pallas_call(
        functools.partial(forward_kernel, places),
        out_shape=(jax.ShapeDtypeStruct((2, TILE, TILE), BF),) * 4,
        in_specs=[pl.BlockSpec(memory_space=SMEM)] * 2 + [vmem] * (1 + len(arrays)),
        out_specs=(vmem,) * 4,
        scratch_shapes=[VMEM((2 * NX * NZ * NY, TILE, TILE), BF)],
        compiler_params=pltpu.CompilerParams(vmem_limit_bytes=24 * 2**20),
        cost_estimate=pl.CostEstimate(flops=2 * rows * slots * TILE**3, bytes_accessed=11 * 2**20, transcendentals=0),
        name="forward",
    )(rep, meta, edges, *arrays)


def middle_kernel(rep_ref, p0, p1, p2, p3, weight_ref, bias_ref, cot_ref, hidden_ref, slope_ref, mine_ref, theirs_ref):
    agg = add32(*[jnp.concatenate([p[0], p[1]], axis=0) for p in (p0, p1, p2, p3)])
    weight = weight_ref[...]
    preact = (
        jnp.dot(agg, weight.astype(F32), preferred_element_type=F32, precision=lax.Precision.HIGHEST)
        + bias_ref[...]
    )
    gate = jax.nn.sigmoid(preact)
    hidden_ref[...] = (preact * gate).astype(BF)
    outgrad = (cot_ref[...].astype(F32) * gate * (1.0 + preact * (1.0 - gate))).astype(BF)
    slope = lax.dot_general(weight, outgrad, (((1,), (1,)), ((), ())), preferred_element_type=F32).astype(BF)
    for i in range(slope_ref.shape[0]):
        slope_ref[i] = slope[:, i * TILE:(i + 1) * TILE]
    wide = outgrad.astype(F32)
    grad = lax.dot_general(
        agg, wide, (((0,), (0,)), ((), ())), preferred_element_type=F32, precision=lax.Precision.HIGHEST
    )
    bias = jnp.sum(wide, axis=0, keepdims=True)
    for ref, same in ((mine_ref, True), (theirs_ref, False)):
        for half in range(2):

            @pl.when(((rep_ref[0] % 2) == half) == same)
            def _(ref=ref, half=half):
                ref[0:64, :] = grad[half * 64:(half + 1) * 64, 0:TILE]
                ref[64:128, :] = grad[half * 64:(half + 1) * 64, TILE:]

        ref[128:144, :] = jnp.broadcast_to(bias[:, 0:TILE], (16, TILE))
        ref[144:160, :] = jnp.broadcast_to(bias[:, TILE:], (16, TILE))


def middle(rep, parts, weight, bias, cotangent):
    nodes, width = cotangent.shape
    vmem = pl.BlockSpec(memory_space=VMEM)
    half = jax.ShapeDtypeStruct((160, TILE), F32)
    return pl.pallas_call(
        middle_kernel,
        out_shape=(
            jax.ShapeDtypeStruct((nodes, width), BF),
            jax.ShapeDtypeStruct((nodes // TILE, TILE, TILE), BF),
            half,
            half,
        ),
        in_specs=[pl.BlockSpec(memory_space=SMEM)] + [vmem] * 7,
        out_specs=(vmem,) * 4,
        compiler_params=pltpu.CompilerParams(vmem_limit_bytes=16 * 2**20),
        name="middle",
    )(rep, *parts, weight, bias.reshape(1, -1), cotangent)


def backward_kernel(places, rep_ref, meta_ref, edges, s0, s1, s2, s3, *rest):
    outs, totals, slope_ref = rest[:-2], rest[-2], rest[-1]
    for q, part in enumerate((s0, s1, s2, s3)):
        for i in range(2):
            slope_ref[(rep_ref[0] ^ q) * 2 + i] = part[i]
    rows, _, slots = edges.shape[:3]

    def clear(i, carry):
        totals[pl.ds(i * 8, 8)] = jnp.zeros((8, TILE, TILE), F32)
        return carry

    lax.fori_loop(0, totals.shape[0] // 8, clear, 0)

    def body(t, count, size):
        slope = slope_ref[t]
        for g in range(size // GROUP):
            which = range(g * GROUP, (g + 1) * GROUP)
            tiles = [live_tile(edges, t, s, count) for s in which]
            terms = jnp.dot(slope, jnp.concatenate(tiles, axis=1), preferred_element_type=F32)
            where = [meta_ref[rows + t * slots + s] for s in which]
            old = [totals[w] for w in where]
            for i, w in enumerate(where):
                totals[w] = old[i] + terms[:, i * TILE:(i + 1) * TILE]

    each_row(meta_ref, edges, body)

    for out, segments in zip(outs, places):
        offset = 0
        for place, size in segments:

            def store(i, carry, out=out, place=place, offset=offset):
                out[pl.ds(offset + i * 4, 4)] = totals[pl.ds(place + i * 4, 4)].astype(out.dtype)
                return carry

            lax.fori_loop(0, size // 4, store, 0)
            offset += size


def backward(rep, meta, edges, slopes, places):
    rows, _, slots = edges.shape[:3]
    vmem = pl.BlockSpec(memory_space=VMEM)
    return pl.pallas_call(
        functools.partial(backward_kernel, places),
        out_shape=tuple(
            jax.ShapeDtypeStruct((sum(size for _, size in segments), TILE, TILE), BF) for segments in places
        ),
        in_specs=[pl.BlockSpec(memory_space=SMEM)] * 2 + [vmem] * 5,
        out_specs=(vmem,) * len(places),
        scratch_shapes=[VMEM((2 * NX * NZ * NY, TILE, TILE), F32), VMEM((rows, TILE, TILE), BF)],
        compiler_params=pltpu.CompilerParams(vmem_limit_bytes=28 * 2**20),
        cost_estimate=pl.CostEstimate(flops=2 * rows * slots * TILE**3, bytes_accessed=15 * 2**20, transcendentals=0),
        name="backward",
    )(rep, meta, edges, *slopes)


def last_kernel(rep_ref, total_ref, mine_ref, theirs_ref, feature_ref, weight_ref, bias_ref):
    for i in range(2):
        feature_ref[0, i * TILE:(i + 1) * TILE, :] = total_ref[i].T.astype(BF)
    for ref, same in ((mine_ref, True), (theirs_ref, False)):
        for half in range(2):

            @pl.when(((rep_ref[0] % 2) == half) == same)
            def _(ref=ref, half=half):
                weight_ref[half * 64:(half + 1) * 64, 0:TILE] = ref[0:64, :]
                weight_ref[half * 64:(half + 1) * 64, TILE:] = ref[64:128, :]
                if half == 0:
                    bias_ref[:, 0:TILE] = ref[128:129, :]
                    bias_ref[:, TILE:] = ref[144:145, :]


def last(rep, total, mine, theirs):
    vmem = pl.BlockSpec(memory_space=VMEM)
    return pl.pallas_call(
        last_kernel,
        out_shape=(
            jax.ShapeDtypeStruct((1, 2 * TILE, TILE), BF),
            jax.ShapeDtypeStruct((TILE, 2 * TILE), F32),
            jax.ShapeDtypeStruct((1, 2 * TILE), F32),
        ),
        in_specs=[pl.BlockSpec(memory_space=SMEM)] + [vmem] * 3,
        out_specs=(vmem, vmem, vmem),
        compiler_params=pltpu.CompilerParams(vmem_limit_bytes=8 * 2**20),
        name="last",
    )(rep, total, mine, theirs)


def gather_features(own):
    own, other = lax.optimization_barrier((own, swap(own, "y")))
    plane = jnp.concatenate([own, shift_x(own, 1), shift_x(own, 2), shift_x(own, -1)])
    spread = jnp.broadcast_to(other[None], (NZ,) + other.shape).reshape(2 * NZ, TILE, TILE)
    line = lax.all_to_all(spread, "z", 0, 0, tiled=True)
    pieces = [(0, plane), (64, line)]
    ahead, behind = shift_x(line, 1), shift_x(line, -1)
    up = down = plane
    for k in (1, 2, 3):
        up, down = shift_z(up, 1), shift_z(down, -1)
        pieces += [(8 * k, up), (8 * (8 - k), down)]
        if k == 2:
            up, ahead, behind = lax.optimization_barrier((up, ahead, behind))
    pieces += [(80, ahead), (112, behind), (96, shift_x(ahead, 1))]
    pieces += [(32, shift_z(up[:4], 1)), (36, shift_z(down[4:], -1))]
    return pieces


OWN_PLACES = tuple(((8 * k, 8),) for k in (4, 3, 5, 2, 6, 1, 7, 0))
OTHER_PLACES = tuple(tuple((64 + 8 * k, 8) for k in ks) for ks in ((4,), (3, 5), (2, 6), (1, 7), (0,)))


def scatter_totals(parts, grad):
    rows = [p.reshape(-1, TILE) for p in parts]
    own, other = rows[:8], rows[8:]
    half, full = 4 * TILE, 8 * TILE
    first = swap(jnp.concatenate([other[0], grad.astype(BF)]), "y")
    wide = add(grad, first[full:])
    last = add(own[0], first[:full])
    up, down = last[:half], last[half:]
    ride_up = ride_down = wide
    grads = [wide]
    for step in range(4):
        moved_up = shift_z(jnp.concatenate([up, ride_up]), 1)
        moved_down = shift_z(down if step == 3 else jnp.concatenate([down, ride_down]), -1)
        met = swap(other[step + 1], "y")
        up, down, met = lax.optimization_barrier((moved_up, moved_down, met))
        size = half if step == 0 else full
        ride_up, ride_down = up[size:], down[size:]
        grads.append(ride_up)
        if step < 3:
            grads.append(ride_down)
        up, down = up[:size], down[:size]
        if step == 3:
            total = add32(own[7], met, up, down)
            break
        here_up, here_down = add32(own[2 * step + 1], met[:full]), add32(own[2 * step + 2], met[full:])
        if step == 0:
            up = jnp.concatenate([add(here_up[:half], up), here_up[half:].astype(BF)])
            down = jnp.concatenate([here_down[:half].astype(BF), add(here_down[half:], down)])
        else:
            up, down = add(here_up, up), add(here_down, down)
    wide = add(*grads)
    part = 2 * TILE
    sent = [total[k * part:(k + 1) * part].astype(BF) for k in (1, 2, 3)]
    got = [shift_x(jnp.concatenate([v, wide]), hop) for v, hop in zip(sent, (1, 2, -1))]
    total = add32(total[:part], *[g[:part] for g in got])
    grad = add32(wide, *[g[part:] for g in got])
    return total.reshape(2, TILE, TILE), grad


def shards(features, weight, bias_vector, edge_tiles, tile_columns, live_counts, cotangent):
    x, z, y = lax.axis_index("x"), lax.axis_index("z"), lax.axis_index("y")
    rep = (lax.axis_index("near") * 2 + lax.axis_index("core")).reshape(1)
    columns = tile_columns.reshape(-1)
    owner, which = columns // 2, columns % 2
    ox, oz, oy = owner // (NZ * NY), (owner // NY) % NZ, owner % NY

    def places(dx, dz, elsewhere):
        return (jnp.where(oy == y, dz * NX + dx, 32 + elsewhere) * 2 + which).astype(jnp.int32)

    counts = live_counts.reshape(-1)
    behind = jnp.concatenate([counts, places((x - ox) % NX, (z - oz) % NZ, (x - ox) % NX * NZ + oz)])
    ahead = jnp.concatenate([counts, places((ox - x) % NX, (oz - z) % NZ, (oz - z) % NZ * NX + (ox - x) % NX)])

    with jax.named_scope("gather"):
        pieces = gather_features(features.reshape(2, TILE, TILE))
    partial = forward(rep, behind, edge_tiles, pieces)
    with jax.named_scope("sections"):
        parts = [
            partial[0],
            swap(partial[1], "core"),
            swap(partial[2], "near"),
            swap(partial[3], "near", "core"),
        ]
    hidden_out, slope, mine, theirs = middle(rep, parts, weight, bias_vector, cotangent)
    with jax.named_scope("slopes"):
        slopes = [slope, swap(slope, "core"), swap(slope, "near"), swap(slope, "near", "core")]
    with jax.named_scope("weights"):
        mine = mine + swap(theirs, "core")
        grad = mine + swap(mine, "near")
    totals = backward(rep, ahead, edge_tiles, slopes, OWN_PLACES + OTHER_PLACES)
    with jax.named_scope("scatter"):
        total, grad = scatter_totals(totals, grad)
        halves = [grad, swap(grad, "core")]
    feature_grad, weight_grad, bias_grad = last(rep, total, *halves)
    return hidden_out, feature_grad, weight_grad, bias_grad.reshape(-1)


def solution(mesh):
    grid = Mesh(mesh.devices.reshape(NX, NZ, NY, 2, 2), ("x", "z", "y", "near", "core"))
    row, rep = ("x", "z", "y"), ("near", "core")
    in_specs = (
        P(rep, row, None),
        P(),
        P(),
        P(row, rep, None, None, None),
        P(row, rep, None),
        P(row, rep),
        P(row + rep, None),
    )
    out_specs = (P(row + rep, None), P(rep, row, None), P(), P())
    return jax.shard_map(shards, mesh=grid, in_specs=in_specs, out_specs=out_specs, check_vma=False)
```

```python
import functools

import jax
import jax.numpy as jnp
from jax import lax
from jax.experimental import pallas as pl
from jax.experimental.pallas import tpu as pltpu
from jax.sharding import Mesh
from jax.sharding import PartitionSpec as P

NX, NZ, NY = 4, 8, 2
TILE = 128
GROUP = 6
BF = jnp.bfloat16
F32 = jnp.float32
VMEM = pltpu.VMEM
SMEM = pltpu.SMEM


def shift_x(value, k):
    return lax.ppermute(value, "x", [(i, (i + k) % NX) for i in range(NX)])


def shift_z(value, k):
    return lax.ppermute(value, "z", [(i, (i + k) % NZ) for i in range(NZ)])


def swap(value, *axes):
    pairs = [(i, (1 << len(axes)) - 1 - i) for i in range(1 << len(axes))]
    return lax.ppermute(value, axes, pairs)


def add32(*values):
    total = values[0].astype(F32)
    for value in values[1:]:
        total = total + value.astype(F32)
    return total


def add(*values):
    return add32(*values).astype(BF)


def each_row(meta_ref, edges, body):
    rows, _, slots = edges.shape[:3]

    def row(t, carry):
        count = meta_ref[t]

        @pl.when(count > GROUP)
        def _():
            body(t, count, slots)

        @pl.when(count <= GROUP)
        def _():
            body(t, count, GROUP)

        return carry

    lax.fori_loop(0, rows, row, 0)


def live_tile(edges, t, s, count):
    tile = edges[t, 0, s]
    return jnp.where(s < count, tile, jnp.zeros_like(tile))


def forward_kernel(places, rep_ref, meta_ref, edges, *rest):
    pieces = rest[: len(places)]
    outs, table = rest[len(places):-1], rest[-1]
    rows, _, slots = edges.shape[:3]
    for piece, (place, size) in zip(pieces, places):

        unit = min(size, 8)

        def copy(i, carry, piece=piece, place=place, unit=unit):
            table[pl.ds(place + i * unit, unit)] = piece[pl.ds(i * unit, unit)]
            return carry

        lax.fori_loop(0, size // unit, copy, 0)

    def body(t, count, size):
        left = [live_tile(edges, t, s, count) for s in range(size)]
        right = [table[meta_ref[rows + t * slots + s]] for s in range(size)]
        total = jnp.dot(
            jnp.concatenate(left, axis=1), jnp.concatenate(right, axis=0), preferred_element_type=F32
        ).astype(BF)
        for q in range(len(outs)):

            @pl.when((t // 2) ^ rep_ref[0] == q)
            def _(q=q):
                outs[q][t % 2] = total

    each_row(meta_ref, edges, body)


def forward(rep, meta, edges, pieces):
    places = tuple((place, piece.shape[0]) for place, piece in pieces)
    arrays = [piece for _, piece in pieces]
    rows, _, slots = edges.shape[:3]
    vmem = pl.BlockSpec(memory_space=VMEM)
    return pl.pallas_call(
        functools.partial(forward_kernel, places),
        out_shape=(jax.ShapeDtypeStruct((2, TILE, TILE), BF),) * 4,
        in_specs=[pl.BlockSpec(memory_space=SMEM)] * 2 + [vmem] * (1 + len(arrays)),
        out_specs=(vmem,) * 4,
        scratch_shapes=[VMEM((2 * NX * NZ * NY, TILE, TILE), BF)],
        compiler_params=pltpu.CompilerParams(vmem_limit_bytes=24 * 2**20),
        cost_estimate=pl.CostEstimate(flops=2 * rows * slots * TILE**3, bytes_accessed=11 * 2**20, transcendentals=0),
        name="forward",
    )(rep, meta, edges, *arrays)


def middle_kernel(rep_ref, p0, p1, p2, p3, weight_ref, bias_ref, cot_ref, hidden_ref, slope_ref, mine_ref, theirs_ref):
    agg = add32(*[jnp.concatenate([p[0], p[1]], axis=0) for p in (p0, p1, p2, p3)])
    weight = weight_ref[...]
    preact = (
        jnp.dot(agg, weight.astype(F32), preferred_element_type=F32, precision=lax.Precision.HIGHEST)
        + bias_ref[...]
    )
    gate = jax.nn.sigmoid(preact)
    hidden_ref[...] = (preact * gate).astype(BF)
    outgrad = (cot_ref[...].astype(F32) * gate * (1.0 + preact * (1.0 - gate))).astype(BF)
    slope = lax.dot_general(weight, outgrad, (((1,), (1,)), ((), ())), preferred_element_type=F32).astype(BF)
    for i in range(slope_ref.shape[0]):
        slope_ref[i] = slope[:, i * TILE:(i + 1) * TILE]
    wide = outgrad.astype(F32)
    grad = lax.dot_general(
        agg, wide, (((0,), (0,)), ((), ())), preferred_element_type=F32, precision=lax.Precision.HIGHEST
    )
    bias = jnp.sum(wide, axis=0, keepdims=True)
    for ref, same in ((mine_ref, True), (theirs_ref, False)):
        for half in range(2):

            @pl.when(((rep_ref[0] % 2) == half) == same)
            def _(ref=ref, half=half):
                ref[0:64, :] = grad[half * 64:(half + 1) * 64, 0:TILE]
                ref[64:128, :] = grad[half * 64:(half + 1) * 64, TILE:]

        ref[128:144, :] = jnp.broadcast_to(bias[:, 0:TILE], (16, TILE))
        ref[144:160, :] = jnp.broadcast_to(bias[:, TILE:], (16, TILE))


def middle(rep, parts, weight, bias, cotangent):
    nodes, width = cotangent.shape
    vmem = pl.BlockSpec(memory_space=VMEM)
    half = jax.ShapeDtypeStruct((160, TILE), F32)
    return pl.pallas_call(
        middle_kernel,
        out_shape=(
            jax.ShapeDtypeStruct((nodes, width), BF),
            jax.ShapeDtypeStruct((nodes // TILE, TILE, TILE), BF),
            half,
            half,
        ),
        in_specs=[pl.BlockSpec(memory_space=SMEM)] + [vmem] * 7,
        out_specs=(vmem,) * 4,
        compiler_params=pltpu.CompilerParams(vmem_limit_bytes=16 * 2**20),
        name="middle",
    )(rep, *parts, weight, bias.reshape(1, -1), cotangent)


def backward_kernel(places, rep_ref, meta_ref, edges, s0, s1, s2, s3, *rest):
    outs, totals, slope_ref = rest[:-2], rest[-2], rest[-1]
    for q, part in enumerate((s0, s1, s2, s3)):
        for i in range(2):
            slope_ref[(rep_ref[0] ^ q) * 2 + i] = part[i]
    rows, _, slots = edges.shape[:3]

    def clear(i, carry):
        totals[pl.ds(i * 8, 8)] = jnp.zeros((8, TILE, TILE), F32)
        return carry

    lax.fori_loop(0, totals.shape[0] // 8, clear, 0)

    def body(t, count, size):
        slope = slope_ref[t]
        for g in range(size // GROUP):
            which = range(g * GROUP, (g + 1) * GROUP)
            tiles = [live_tile(edges, t, s, count) for s in which]
            terms = jnp.dot(slope, jnp.concatenate(tiles, axis=1), preferred_element_type=F32)
            where = [meta_ref[rows + t * slots + s] for s in which]
            old = [totals[w] for w in where]
            for i, w in enumerate(where):
                totals[w] = old[i] + terms[:, i * TILE:(i + 1) * TILE]

    each_row(meta_ref, edges, body)

    for out, segments in zip(outs, places):
        offset = 0
        for place, size in segments:

            def store(i, carry, out=out, place=place, offset=offset):
                out[pl.ds(offset + i * 8, 8)] = totals[pl.ds(place + i * 8, 8)].astype(out.dtype)
                return carry

            lax.fori_loop(0, size // 8, store, 0)
            offset += size


def backward(rep, meta, edges, slopes, places):
    rows, _, slots = edges.shape[:3]
    vmem = pl.BlockSpec(memory_space=VMEM)
    return pl.pallas_call(
        functools.partial(backward_kernel, places),
        out_shape=tuple(
            jax.ShapeDtypeStruct((sum(size for _, size in segments), TILE, TILE), BF) for segments in places
        ),
        in_specs=[pl.BlockSpec(memory_space=SMEM)] * 2 + [vmem] * 5,
        out_specs=(vmem,) * len(places),
        scratch_shapes=[VMEM((2 * NX * NZ * NY, TILE, TILE), F32), VMEM((rows, TILE, TILE), BF)],
        compiler_params=pltpu.CompilerParams(vmem_limit_bytes=28 * 2**20),
        cost_estimate=pl.CostEstimate(flops=2 * rows * slots * TILE**3, bytes_accessed=15 * 2**20, transcendentals=0),
        name="backward",
    )(rep, meta, edges, *slopes)


def last_kernel(rep_ref, total_ref, mine_ref, theirs_ref, feature_ref, weight_ref, bias_ref):
    for i in range(2):
        feature_ref[0, i * TILE:(i + 1) * TILE, :] = total_ref[i].T.astype(BF)
    for ref, same in ((mine_ref, True), (theirs_ref, False)):
        for half in range(2):

            @pl.when(((rep_ref[0] % 2) == half) == same)
            def _(ref=ref, half=half):
                weight_ref[half * 64:(half + 1) * 64, 0:TILE] = ref[0:64, :]
                weight_ref[half * 64:(half + 1) * 64, TILE:] = ref[64:128, :]
                if half == 0:
                    bias_ref[:, 0:TILE] = ref[128:129, :]
                    bias_ref[:, TILE:] = ref[144:145, :]


def last(rep, total, mine, theirs):
    vmem = pl.BlockSpec(memory_space=VMEM)
    return pl.pallas_call(
        last_kernel,
        out_shape=(
            jax.ShapeDtypeStruct((1, 2 * TILE, TILE), BF),
            jax.ShapeDtypeStruct((TILE, 2 * TILE), F32),
            jax.ShapeDtypeStruct((1, 2 * TILE), F32),
        ),
        in_specs=[pl.BlockSpec(memory_space=SMEM)] + [vmem] * 3,
        out_specs=(vmem, vmem, vmem),
        compiler_params=pltpu.CompilerParams(vmem_limit_bytes=8 * 2**20),
        name="last",
    )(rep, total, mine, theirs)


def gather_features(own):
    own, other = lax.optimization_barrier((own, swap(own, "y")))
    plane = jnp.concatenate([own, shift_x(own, 1), shift_x(own, 2), shift_x(own, -1)])
    spread = jnp.broadcast_to(other[None], (NZ,) + other.shape).reshape(2 * NZ, TILE, TILE)
    line = lax.all_to_all(spread, "z", 0, 0, tiled=True)
    pieces = [(0, plane), (64, line)]
    ahead, behind = shift_x(line, 1), shift_x(line, -1)
    up = down = plane
    for k in (1, 2, 3):
        up, down = shift_z(up, 1), shift_z(down, -1)
        pieces += [(8 * k, up), (8 * (8 - k), down)]
        if k == 2:
            up, ahead, behind = lax.optimization_barrier((up, ahead, behind))
    pieces += [(80, ahead), (112, behind), (96, shift_x(ahead, 1))]
    pieces += [(32, shift_z(up[:4], 1)), (36, shift_z(down[4:], -1))]
    return pieces


OWN_PLACES = tuple(((8 * k, 8),) for k in (4, 3, 5, 2, 6, 1, 7, 0))
OTHER_PLACES = tuple(tuple((64 + 8 * k, 8) for k in ks) for ks in ((4,), (3, 5), (2, 6), (1, 7), (0,)))


def scatter_totals(parts, grad):
    rows = [p.reshape(-1, TILE) for p in parts]
    own, other = rows[:8], rows[8:]
    half, full = 4 * TILE, 8 * TILE
    first = swap(jnp.concatenate([other[0], grad.astype(BF)]), "y")
    wide = add(grad, first[full:])
    last = add(own[0], first[:full])
    up, down = last[:half], last[half:]
    ride_up = ride_down = wide
    grads = [wide]
    for step in range(4):
        moved_up = shift_z(jnp.concatenate([up, ride_up]), 1)
        moved_down = shift_z(down if step == 3 else jnp.concatenate([down, ride_down]), -1)
        met = swap(other[step + 1], "y")
        up, down, met = lax.optimization_barrier((moved_up, moved_down, met))
        size = half if step == 0 else full
        ride_up, ride_down = up[size:], down[size:]
        grads.append(ride_up)
        if step < 3:
            grads.append(ride_down)
        up, down = up[:size], down[:size]
        if step == 3:
            total = add32(own[7], met, up, down)
            break
        here_up, here_down = add32(own[2 * step + 1], met[:full]), add32(own[2 * step + 2], met[full:])
        if step == 0:
            up = jnp.concatenate([add(here_up[:half], up), here_up[half:].astype(BF)])
            down = jnp.concatenate([here_down[:half].astype(BF), add(here_down[half:], down)])
        else:
            up, down = add(here_up, up), add(here_down, down)
    wide = add(*grads)
    part = 2 * TILE
    sent = [total[k * part:(k + 1) * part].astype(BF) for k in (1, 2, 3)]
    got = [shift_x(jnp.concatenate([v, wide]), hop) for v, hop in zip(sent, (1, 2, -1))]
    total = add32(total[:part], *[g[:part] for g in got])
    grad = add32(wide, *[g[part:] for g in got])
    return total.reshape(2, TILE, TILE), grad


def shards(features, weight, bias_vector, edge_tiles, tile_columns, live_counts, cotangent):
    x, z, y = lax.axis_index("x"), lax.axis_index("z"), lax.axis_index("y")
    rep = (lax.axis_index("near") * 2 + lax.axis_index("core")).reshape(1)
    columns = tile_columns.reshape(-1)
    owner, which = columns // 2, columns % 2
    ox, oz, oy = owner // (NZ * NY), (owner // NY) % NZ, owner % NY

    def places(dx, dz, elsewhere):
        return (jnp.where(oy == y, dz * NX + dx, 32 + elsewhere) * 2 + which).astype(jnp.int32)

    counts = live_counts.reshape(-1)
    behind = jnp.concatenate([counts, places((x - ox) % NX, (z - oz) % NZ, (x - ox) % NX * NZ + oz)])
    ahead = jnp.concatenate([counts, places((ox - x) % NX, (oz - z) % NZ, (oz - z) % NZ * NX + (ox - x) % NX)])

    with jax.named_scope("gather"):
        pieces = gather_features(features.reshape(2, TILE, TILE))
    partial = forward(rep, behind, edge_tiles, pieces)
    with jax.named_scope("sections"):
        parts = [
            partial[0],
            swap(partial[1], "core"),
            swap(partial[2], "near"),
            swap(partial[3], "near", "core"),
        ]
    hidden_out, slope, mine, theirs = middle(rep, parts, weight, bias_vector, cotangent)
    with jax.named_scope("slopes"):
        slopes = [slope, swap(slope, "core"), swap(slope, "near"), swap(slope, "near", "core")]
    with jax.named_scope("weights"):
        mine = mine + swap(theirs, "core")
        grad = mine + swap(mine, "near")
    totals = backward(rep, ahead, edge_tiles, slopes, OWN_PLACES + OTHER_PLACES)
    with jax.named_scope("scatter"):
        total, grad = scatter_totals(totals, grad)
        halves = [grad, swap(grad, "core")]
    feature_grad, weight_grad, bias_grad = last(rep, total, *halves)
    return hidden_out, feature_grad, weight_grad, bias_grad.reshape(-1)


def solution(mesh):
    grid = Mesh(mesh.devices.reshape(NX, NZ, NY, 2, 2), ("x", "z", "y", "near", "core"))
    row, rep = ("x", "z", "y"), ("near", "core")
    in_specs = (
        P(rep, row, None),
        P(),
        P(),
        P(row, rep, None, None, None),
        P(row, rep, None),
        P(row, rep),
        P(row + rep, None),
    )
    out_specs = (P(row + rep, None), P(rep, row, None), P(), P())
    return jax.shard_map(shards, mesh=grid, in_specs=in_specs, out_specs=out_specs, check_vma=False)
```
